256 devices in a mesh: px: 32 (over z, y_lo, core), py: 8 (over x, y_hi).
Axes of the slice: x: 4, y: 4 (y_hi: 2, y_lo: 2; y = y_hi * 2 + y_lo), z: 8, core: 2. Of those that a mesh axis runs over, the one named last changes fastest.
Arguments:
- waves: float32 [2, 256, 131072], P(None, None, ('px', 'py')), may hold values from -6 to 6
- col_map: int32 [1024], P(('px', 'py')), may hold values from 0 to 63, as said below
- potential: float32 [128, 128, 128], P(None, 'px', 'py'), may hold values from -6 to 6
- projectors: float32 [2, 256, 131072], P(None, None, ('px', 'py')), may hold values from -0.1875 to 0.1875
- coupling: float32 [32, 8, 8], replicated, may hold values from -4 to 4
Outputs:
- hpsi: float32 [2, 16, 131072], P(None, None, ('px', 'py'))
- correlation: float32 [2, 256, 256], P(None, 'px', 'py')
- energy: float32 [2, 256, 16], P(None, 'px', 'py')
The draws below stay inside these ranges and needn't reach their ends.
Inputs may be any that keep to these rules, and one draw needn't show every extreme that they name: `col_map`: on each device the 4 entries are distinct and ascending.
All inputs are finite; a program needn't handle non-finite values.
Results may differ from the reference program's by a relative error of at most 0.000064.
Values sent between devices are 32-bit elements; how exact they have to be, the bound alone decides.
A program may use at most 64 MiB of HBM per device.

```python
import jax
import jax.numpy as jnp
from jax import lax

NG = 128
NB = 256
BLK = 8
BW = 16
NCOLD = 4
ATOMS = 32
GCUT = 50
NPROJ = 256
NCOLS = 1024
NCOEF = 131072
N_PX = 32
N_PY = 8


def draw_col_map(key, part):
    key = jax.random.fold_in(key, 7)
    x_width = NG // N_PX
    y_width = NG // N_PY
    slots = x_width * y_width
    count = N_PX * N_PY
    slot_ids = jnp.arange(slots, dtype=jnp.int32)

    def one_device(device_key, device):
        xg = device // N_PY + N_PX * (slot_ids // y_width)
        yg = device % N_PY + N_PY * (slot_ids % y_width)
        fx = jnp.where(xg < NG // 2, xg, xg - NG)
        fy = jnp.where(yg < NG // 2, yg, yg - NG)
        inside = jnp.where(fx * fx + fy * fy <= GCUT * GCUT, 1, 0).astype(jnp.int32)
        score = jax.random.permutation(device_key, slots).astype(jnp.int32) + slots * inside
        chosen = lax.top_k(score, NCOLD)[1].astype(jnp.int32)
        return jnp.sort(chosen)
    keys = jax.random.split(key, count)
    return jax.vmap(one_device)(keys, jnp.arange(count, dtype=jnp.int32)).reshape(-1)


def steps_of(rng, shape, cuts, smallest, high):
    level, own = 1.0, jax.random.fold_in(rng, 6)
    for position, blocks in cuts:
        steps = jnp.exp(jax.random.uniform(jax.random.fold_in(own, position), (blocks,), jnp.float32, smallest / len(cuts), high / len(cuts)))
        level = level * jnp.repeat(steps, shape[position] // blocks).reshape([-1 if axis == position else 1 for axis in range(len(shape))])
    return level


def bell_draw(key, dims, spread, most, shards=(), kind=jnp.bfloat16):
    entries = jax.random.normal(key, dims, jnp.float32) * spread
    if len(shards) > 0:
        entries = steps_of(key, dims, shards, -0.22, 0.18) * entries
    return jnp.clip(entries, min=-most, max=most).astype(kind)


def setup_inputs(seed: int = 0) -> dict:
    arg_keys = jax.random.split(jax.random.key(seed), 6)
    return {
        "waves": bell_draw(arg_keys[0], (2, NB, NCOEF), 1.0, 6.0, ((2, 256),), jnp.float32),
        "col_map": draw_col_map(jax.random.fold_in(arg_keys[5], 71), 0),
        "potential": bell_draw(arg_keys[2], (NG, NG, NG), 1.0, 6.0, ((1, 32), (2, 8)), jnp.float32),
        "projectors": bell_draw(arg_keys[3], (2, NPROJ, NCOEF), (1.0 / (NCOEF * NPROJ) ** 0.25), 0.1875, ((2, 256),), jnp.float32),
        "coupling": bell_draw(arg_keys[4], (ATOMS, BLK, BLK), 0.3, 4.0, (), jnp.float32),
    }


def frequency(index):
    return jnp.where(index < NG // 2, index, index - NG).astype(jnp.int32)


def reference(waves, col_map, potential, projectors, coupling):
    highest = lax.Precision.HIGHEST
    y_width = NG // N_PY
    device = jnp.arange(NCOLS, dtype=jnp.int32) // NCOLD
    xpos = ((device // N_PY) + N_PX * (col_map // y_width)).astype(jnp.int32)
    ypos = ((device % N_PY) + N_PY * (col_map % y_width)).astype(jnp.int32)
    freq_x = frequency(xpos)
    freq_y = frequency(ypos)
    freq_z = frequency(jnp.arange(NG, dtype=jnp.int32))
    square = (freq_x * freq_x + freq_y * freq_y)[:, None] + (freq_z * freq_z)[None, :]
    sphere = jnp.where(square <= GCUT * GCUT, 1.0, 0.0).astype(jnp.float32).reshape(NCOEF)
    kinetic = (square.astype(jnp.float32) * (2.0 / (NG * NG))).reshape(NCOEF)
    masked = waves * sphere[None, None, :]
    beta = projectors * sphere[None, None, :]
    window = masked[:, :BW]

    def apply_local(band):
        columns = lax.complex(band[0], band[1]).reshape(NCOLS, NG)
        grid = jnp.zeros((NG, NG, NG), columns.dtype).at[xpos, ypos, :].set(columns)
        image = jnp.fft.fftn(jnp.fft.ifftn(grid, norm="ortho") * potential, norm="ortho")
        picked = image[xpos, ypos, :].reshape(NCOEF)
        return jnp.stack([jnp.real(picked), jnp.imag(picked)])

    local = jnp.swapaxes(lax.map(apply_local, jnp.swapaxes(window, 0, 1)), 0, 1)
    wave_re = window[0]
    wave_im = window[1]
    beta_re = beta[0]
    beta_im = beta[1]
    proj_re = jnp.dot(beta_re, wave_re.T, precision=highest) + jnp.dot(beta_im, wave_im.T, precision=highest)
    proj_im = jnp.dot(beta_re, wave_im.T, precision=highest) - jnp.dot(beta_im, wave_re.T, precision=highest)
    sym = 0.5 * (coupling + jnp.swapaxes(coupling, 1, 2))
    coef_re = jnp.einsum("aij,ajb->aib", sym, proj_re.reshape(ATOMS, BLK, BW), precision=highest).reshape(NPROJ, BW)
    coef_im = jnp.einsum("aij,ajb->aib", sym, proj_im.reshape(ATOMS, BLK, BW), precision=highest).reshape(NPROJ, BW)
    nonlocal_re = jnp.dot(coef_re.T, beta_re, precision=highest) - jnp.dot(coef_im.T, beta_im, precision=highest)
    nonlocal_im = jnp.dot(coef_im.T, beta_re, precision=highest) + jnp.dot(coef_re.T, beta_im, precision=highest)
    hpsi_re = kinetic[None, :] * wave_re + sphere[None, :] * local[0] + nonlocal_re
    hpsi_im = kinetic[None, :] * wave_im + sphere[None, :] * local[1] + nonlocal_im
    all_re = masked[0]
    all_im = masked[1]
    over_re = jnp.dot(all_re, all_re.T, precision=highest) + jnp.dot(all_im, all_im.T, precision=highest)
    over_im = jnp.dot(all_re, all_im.T, precision=highest) - jnp.dot(all_im, all_re.T, precision=highest)
    ham_re = jnp.dot(all_re, hpsi_re.T, precision=highest) + jnp.dot(all_im, hpsi_im.T, precision=highest)
    ham_im = jnp.dot(all_re, hpsi_im.T, precision=highest) - jnp.dot(all_im, hpsi_re.T, precision=highest)
    scale = 1.0 / NCOEF
    hpsi = jnp.stack([hpsi_re, hpsi_im])
    correlation = jnp.stack([over_re, over_im]) * scale
    energy = jnp.stack([ham_re, ham_im]) * scale
    return hpsi, correlation, energy
```

```python
import math

import jax
import jax.numpy as jnp
import numpy as np
from jax import lax
from jax.experimental import pallas as pl
from jax.experimental.pallas import tpu as pltpu
from jax.sharding import PartitionSpec as P

NG = 128
NB = 256
BW = 16
NCOLD = 4
GCUT = 50
NPX = 32
NPY = 8
NDEV = NPX * NPY
LOCAL = NCOLD * NG
MESH = pl.DeviceIdType.MESH
F32 = jnp.float32
BF16 = jnp.bfloat16


def dft_tables():
    index = np.arange(NG)
    angle = (index[:, None] * index[None, :] % NG) * (2.0 * math.pi / NG)
    cosine = np.cos(angle) / math.sqrt(NG)
    sine = np.sin(angle) / math.sqrt(NG)
    left = np.block([[cosine, -sine], [sine, cosine]])
    right = np.block([[cosine, sine], [-sine, cosine]])
    parts = []
    for table in (left, right):
        high = table.astype(jnp.bfloat16)
        low = (table - high.astype(np.float64)).astype(jnp.bfloat16)
        parts += [high, low]
    return np.stack(parts)


def split(x):
    high = x.astype(BF16)
    return high, (x - high.astype(F32)).astype(BF16)


def product(a, b, transposed=False):
    dims = (((1,), (1 if transposed else 0,)), ((), ()))

    def dot(u, v):
        return lax.dot_general(u, v, dims, preferred_element_type=F32)

    return dot(a[0], b[0]) + (dot(a[0], b[1]) + dot(a[1], b[0]))


def pair(ref, *index):
    return ref[(0, *index)], ref[(1, *index)]


def far_first(digit, half):
    odd = lax.rem(digit, 2)
    return half + (1 - 2 * odd) * lax.div(digit + 1, 2)


def partner_px(k, p):
    z = lax.rem(lax.div(p, 4) + far_first(lax.div(k, 4), 4), 8)
    y_lo = lax.rem(lax.div(p, 2) + 1 + lax.rem(lax.div(k, 2), 2), 2)
    core = lax.rem(p + 1 + lax.rem(k, 2), 2)
    return z * 4 + y_lo * 2 + core


def partner_py(k, q):
    x = lax.rem(lax.div(q, 2) + far_first(lax.div(k, 2), 2), 4)
    y_hi = lax.rem(q + 1 + lax.rem(k, 2), 2)
    return x * 2 + y_hi


def partner(k, p, q):
    p_digit = lax.div(k, 32) * 4 + lax.rem(k, 4)
    q_digit = lax.rem(lax.div(k, 4), 8)
    return partner_px(p_digit, p), partner_py(q_digit, q)


def remote(src, dst, sems, place):
    return pltpu.make_async_remote_copy(
        src_ref=src,
        dst_ref=dst,
        send_sem=sems.at[0],
        recv_sem=sems.at[1],
        device_id=place,
        device_id_type=MESH,
    )


def wait_bytes(ref, sem):
    pltpu.make_async_copy(ref, ref, sem).wait()


def kernel(
    waves_hbm,
    col_hbm,
    pot_hbm,
    beta_hbm,
    coup_hbm,
    mats_hbm,
    hpsi_ref,
    corr_ref,
    energy_ref,
    waves,
    beta,
    pot,
    coup,
    mats,
    col,
    phi_s,
    beta_s,
    sym_s,
    fwd_send,
    fwd_recv,
    pot_send,
    pot_recv,
    ca_send,
    ca_recv,
    cb_send,
    cb_recv,
    back_send,
    back_recv,
    en_send,
    en_recv,
    unpack,
    field,
    grid,
    picked,
    ham,
    load_sems,
    own_sems,
    fwd_sems,
    pot_sems,
    ca_sems,
    cb_sems,
    back_sems,
    en_sems,
):
    p = lax.axis_index("px")
    q = lax.axis_index("py")
    z_low = lax.div(p, 2)
    half = lax.rem(p, 2)
    owner = half * NG + q * 16 + z_low
    slot = q * NPX + p

    barrier = pltpu.get_barrier_semaphore()

    def greet(k, carry):
        pl.semaphore_signal(barrier, inc=1, device_id=partner(k, p, q), device_id_type=MESH)
        return carry

    loads = [
        (waves_hbm.at[:, pl.ds(0, BW)], waves.at[:, pl.ds(0, BW)]),
        (mats_hbm, mats),
        (col_hbm, col),
        (beta_hbm, beta),
        (waves_hbm.at[:, pl.ds(BW, NB - BW)], waves.at[:, pl.ds(BW, NB - BW)]),
        (pot_hbm, pot),
        (coup_hbm, coup),
    ]
    loads = [pltpu.make_async_copy(s, d, load_sems.at[i]) for i, (s, d) in enumerate(loads)]
    for load in loads:
        load.start()
    lax.fori_loop(0, NDEV - 1, greet, 0, unroll=5)

    lane = lax.broadcasted_iota(jnp.int32, (1, NG), 1)

    loads[0].wait()
    loads[1].wait()
    loads[2].wait()
    z_freq = jnp.where(lane < NG // 2, lane, lane - NG)
    spheres = []
    kinetics = []
    cols = jnp.zeros((1, NG), F32)
    for j in range(NCOLD):
        place = col[j]
        cols = jnp.where(lane == 96 + j, place.astype(F32), cols)
        x = p + NPX * lax.div(place, 16)
        y = q + NPY * lax.rem(place, 16)
        fx = jnp.where(x < NG // 2, x, x - NG)
        fy = jnp.where(y < NG // 2, y, y - NG)
        square = fx * fx + fy * fy + z_freq * z_freq
        spheres.append(jnp.where(square <= GCUT * GCUT, 1.0, 0.0).astype(F32))
        kinetics.append(square.astype(F32) * (2.0 / (NG * NG)))
    sphere = jnp.concatenate(spheres, axis=1)
    kinetic = jnp.concatenate(kinetics, axis=1)

    psi_re = waves[0, 0:BW, :] * sphere
    psi_im = waves[1, 0:BW, :] * sphere
    rows = []
    for h in range(2):
        for part in range(2):
            for j in range(NCOLD):
                re = psi_re[h * 8 : h * 8 + 8, j * NG : j * NG + NG]
                im = psi_im[h * 8 : h * 8 + 8, j * NG : j * NG + NG]
                rows.append(jnp.concatenate([re, -im] if part == 0 else [im, re], axis=1))
    z_rows = product(pair(mats.at[pl.ds(2, 2)], slice(0, NG)), split(jnp.concatenate(rows)), True)

    loads[3].wait()
    for part in range(2):
        high, low = split(beta[part] * sphere)
        beta_s[0, part * NB : part * NB + NB, :] = high
        beta_s[1, part * NB : part * NB + NB, :] = low
    zeros = jnp.zeros((32, LOCAL), F32)
    with_re = split(jnp.concatenate([zeros, zeros, psi_re, psi_im, zeros]))
    with_im = split(jnp.concatenate([zeros, zeros, psi_im, -psi_re, zeros]))
    partial = product(pair(beta_s, slice(0, NB)), with_re, True) + product(
        pair(beta_s, slice(NB, 2 * NB)), with_im, True
    )
    for h in range(2):
        part = pltpu.roll(z_rows, 64, 1) if h else z_rows
        rows = jnp.where(lane < 64, part, partial[h * NG : h * NG + NG]) + cols
        fwd_send[h * NG : h * NG + NG, 0, :] = rows

    loads[5].wait()
    for y in range(4):
        pot_send[:, y, :] = pot[:, y, :].T

    pl.semaphore_wait(barrier, NDEV - 1)

    def send_forward(k, carry):
        to_p, to_q = partner(k, p, q)
        row = lax.rem(to_p, 2) * NG + to_q * 16 + lax.div(to_p, 2)
        remote(fwd_send.at[row], fwd_recv.at[slot], fwd_sems, (to_p, to_q)).start()
        return carry

    lax.fori_loop(0, NDEV - 1, send_forward, 0, unroll=5)
    own_forward = pltpu.make_async_copy(fwd_send.at[owner], fwd_recv.at[slot], own_sems.at[0])
    own_forward.start()

    def send_potential(k, carry):
        to_p = partner_px(k, p)
        remote(pot_send.at[lax.div(to_p, 2)], pot_recv.at[p], pot_sems, (to_p, q)).start()
        return carry

    lax.fori_loop(0, NPX - 1, send_potential, 0)
    own_pot = pltpu.make_async_copy(pot_send.at[z_low], pot_recv.at[p], own_sems.at[1])
    own_pot.start()

    loads[4].wait()
    for part in range(2):
        high, low = split(waves[part] * sphere)
        phi_s[0, :, part * LOCAL : part * LOCAL + LOCAL] = high
        phi_s[1, :, part * LOCAL : part * LOCAL + LOCAL] = low
    phi = pair(phi_s)
    turned = tuple(jnp.concatenate([-x[:, LOCAL:], x[:, :LOCAL]], axis=1) for x in phi)
    ca_send[:, 0] = product(phi, phi, True).reshape(NPY, 32, NB)
    ca_send[:, 1] = product(phi, turned, True).reshape(NPY, 32, NB)

    def send_corr_a(k, carry):
        to_q = partner_py(k, q)
        remote(ca_send.at[to_q], ca_recv.at[q], ca_sems, (p, to_q)).start()
        return carry

    lax.fori_loop(0, NPY - 1, send_corr_a, 0)
    own_ca = pltpu.make_async_copy(ca_send.at[q], ca_recv.at[q], own_sems.at[2])
    own_ca.start()

    loads[6].wait()
    blk_row = lax.broadcasted_iota(jnp.int32, (8, NB), 0)
    blk_lane = lax.broadcasted_iota(jnp.int32, (8, NB), 1)
    spread = jnp.where(lax.rem(blk_lane, 8) == blk_row, 1.0, 0.0).astype(F32)
    wide = jnp.dot(coup[...], spread, precision=lax.Precision.HIGHEST, preferred_element_type=F32)
    sym_row = lax.broadcasted_iota(jnp.int32, (NB, NB), 0)
    sym_lane = lax.broadcasted_iota(jnp.int32, (NB, NB), 1)
    wide = jnp.where(lax.div(sym_row, 8) == lax.div(sym_lane, 8), wide, 0.0)
    high, low = split(0.5 * (wide + wide.T))
    sym_s[0] = high
    sym_s[1] = low
    picked[...] = jnp.zeros((NPY * NG, NG), F32)

    own_forward.wait()
    wait_bytes(fwd_recv.at[pl.ds(0, NDEV - 1)], fwd_sems.at[1])
    proj_sum = jnp.zeros((NPX, NG), F32)
    for s in range(NPY):
        block = fwd_recv[s * NPX : s * NPX + NPX, 0, :]
        proj_sum = proj_sum + block
        unpack[s * NG : s * NG + NG, :] = jnp.concatenate([block] * 4).T
    proj_sum = jnp.sum(proj_sum, axis=0, keepdims=True)
    proj_row = jnp.where((lane >= 64) & (lane < 96), proj_sum, 0.0)
    x_slot = lax.div(lane, 32).astype(F32) * 16.0
    y_slot = lax.broadcasted_iota(jnp.int32, (16, NPY, NG), 0).astype(F32)
    found = []
    for j in range(NCOLD):
        place = unpack[pl.ds(96 + j, NPY, stride=NG), :] - x_slot
        found.append(y_slot == place[None])
    for b in range(8):
        for part in range(2):
            plane = jnp.zeros((16, NPY, NG), F32)
            for j in range(NCOLD):
                value = unpack[pl.ds(part * 32 + j * 8 + b, NPY, stride=NG), :]
                plane = jnp.where(found[j], value[None], plane)
            field[part * NG : part * NG + NG, b * NG : b * NG + NG] = plane.reshape(NG, NG)

    own_pot.wait()
    wait_bytes(pot_recv.at[pl.ds(0, NPX - 1)], pot_sems.at[1])
    potential = pot_recv[...].reshape(NG, NG)
    potential = jnp.concatenate([potential, potential], axis=1)
    mat_a = pair(mats.at[pl.ds(0, 2)])
    mat_b = pair(mats.at[pl.ds(2, 2)])
    for c in range(4):
        two = slice(c * 256, c * 256 + 256)
        lines = product(mat_a, split(field[:, two]))
        planes = []
        for b in range(2):
            part = lines[:, b * NG : b * NG + NG]
            planes.append(jnp.concatenate([part[:NG], part[NG:]], axis=1))
        real = product(split(jnp.concatenate(planes)), mat_b)
        real = real * jnp.concatenate([potential, potential])
        back = product(split(real), mat_a)
        columns = []
        for b in range(2):
            part = back[b * NG : b * NG + NG]
            columns.append(jnp.concatenate([part[:, :NG], part[:, NG:]]))
        grid[:, two] = product(mat_b, split(jnp.concatenate(columns, axis=1)))
    for b in range(8):
        for part in range(2):
            plane = grid[part * NG : part * NG + NG, b * NG : b * NG + NG].reshape(16, NPY, NG)
            for j in range(NCOLD):
                value = jnp.sum(jnp.where(found[j], plane, 0.0), axis=0)
                picked[pl.ds(part * 32 + j * 8 + b, NPY, stride=NG), :] = value
    for s in range(NPY):
        turned = picked[s * NG : s * NG + NG, :].T
        block = turned[0:32] + turned[32:64] + turned[64:96] + turned[96:128]
        back_send[s * NPX : s * NPX + NPX, 0, :] = block + proj_row

    def send_back(k, carry):
        to_p, to_q = partner(k, p, q)
        remote(
            back_send.at[to_q * NPX + to_p], back_recv.at[owner], back_sems, (to_p, to_q)
        ).start()
        return carry

    lax.fori_loop(0, NDEV - 1, send_back, 0, unroll=5)
    own_back = pltpu.make_async_copy(back_send.at[slot], back_recv.at[owner], own_sems.at[3])
    own_back.start()

    own_ca.wait()
    wait_bytes(ca_recv.at[pl.ds(0, NPY - 1)], ca_sems.at[1])
    total = ca_recv[0]
    for s in range(1, NPY):
        total = total + ca_recv[s]
    total = total.reshape(64, NB)
    total = jnp.concatenate([total, jnp.zeros((64, NB), F32)])
    cb_send[...] = total.T.reshape(NPX, 8, NG)

    def send_corr_b(k, carry):
        to_p = partner_px(k, p)
        remote(cb_send.at[to_p], cb_recv.at[p], cb_sems, (to_p, q)).start()
        return carry

    lax.fori_loop(0, NPX - 1, send_corr_b, 0)
    own_cb = pltpu.make_async_copy(cb_send.at[p], cb_recv.at[p], own_sems.at[4])
    own_cb.start()

    own_back.wait()
    wait_bytes(back_recv.at[pl.ds(0, NDEV - 1)], back_sems.at[1])
    low_rows = back_recv[0:NG, 0, :]
    high_rows = back_recv[NG : 2 * NG, 0, :]
    lines = jnp.where(lane < 64, low_rows, pltpu.roll(high_rows, 64, 1)).T
    lines = product(split(lines), pair(mats.at[pl.ds(2, 2)], slice(0, NG)))
    local_re = []
    local_im = []
    for h in range(2):
        res = [lines[h * 64 + j * 8 : h * 64 + j * 8 + 8] for j in range(4)]
        ims = [lines[h * 64 + 32 + j * 8 : h * 64 + 40 + j * 8] for j in range(4)]
        local_re.append(
            jnp.concatenate([r[:, :NG] + i[:, NG:] for r, i in zip(res, ims)], axis=1)
        )
        local_im.append(
            jnp.concatenate([i[:, :NG] - r[:, NG:] for r, i in zip(res, ims)], axis=1)
        )

    proj = jnp.concatenate([low_rows, high_rows])
    proj = pltpu.roll(proj, 64, 1).T[0:32]
    coef = product(split(proj), pair(sym_s))
    coef_re = coef[0:16]
    coef_im = coef[16:32]
    coef = jnp.concatenate(
        [
            jnp.concatenate([coef_re, -coef_im], axis=1),
            jnp.concatenate([coef_im, coef_re], axis=1),
        ]
    )
    nonlocal_part = product(split(coef), pair(beta_s))
    psi_re = waves[0, 0:BW, :] * sphere
    psi_im = waves[1, 0:BW, :] * sphere
    hpsi_re = kinetic * psi_re + sphere * jnp.concatenate(local_re) + nonlocal_part[0:16]
    hpsi_im = kinetic * psi_im + sphere * jnp.concatenate(local_im) + nonlocal_part[16:32]
    hpsi_ref[0] = hpsi_re
    hpsi_ref[1] = hpsi_im

    rows = []
    for h in range(2):
        re = hpsi_re[h * 8 : h * 8 + 8]
        im = hpsi_im[h * 8 : h * 8 + 8]
        rows.append(jnp.concatenate([re, im], axis=1))
        rows.append(jnp.concatenate([im, -re], axis=1))
    rows = split(jnp.concatenate(rows))
    rows = tuple(jnp.concatenate([x[0:16]] * 8 + [x[16:32]] * 8) for x in rows)
    partial = product(pair(phi_s), rows, True)
    for h in range(2):
        ham[...] = partial[:, h * NG : h * NG + NG]
        block = jnp.zeros((NPX, NG), F32)
        for m in range(8):
            strip = ham[pl.ds(m, NPX, stride=8), :]
            block = jnp.where(lax.div(lane, 16) == m, strip, block)
        en_send[h * NPX : h * NPX + NPX, 0, :] = block

    def send_energy(k, carry):
        to_p, to_q = partner(k, p, q)
        remote(
            en_send.at[lax.div(to_q, 4) * NPX + to_p], en_recv.at[slot], en_sems, (to_p, to_q)
        ).start()
        return carry

    lax.fori_loop(0, NDEV - 1, send_energy, 0, unroll=5)
    own_en = pltpu.make_async_copy(
        en_send.at[lax.div(q, 4) * NPX + p], en_recv.at[slot], own_sems.at[5]
    )
    own_en.start()

    scale = 1.0 / (NDEV * LOCAL)
    own_cb.wait()
    wait_bytes(cb_recv.at[pl.ds(0, NPX - 1)], cb_sems.at[1])
    total = jnp.sum(cb_recv[...], axis=0) * scale
    corr_ref[0] = total[:, 0:32]
    corr_ref[1] = total[:, 32:64]

    own_en.wait()
    wait_bytes(en_recv.at[pl.ds(0, NDEV - 1)], en_sems.at[1])
    total = jnp.zeros((NPX, NG), F32)
    for s in range(NPY):
        total = total + en_recv[s * NPX : s * NPX + NPX, 0, :]
    total = jnp.sum(total, axis=0, keepdims=True) * scale
    m_row = lax.broadcasted_iota(jnp.int32, (8, NG), 0)
    m_lane = lax.broadcasted_iota(jnp.int32, (8, NG), 1)
    mine = jnp.where(lax.div(m_lane, 16) == m_row, total, 0.0)
    for part in range(2):
        n_first = part * 8 + lax.rem(q, 4) * 2
        for n in range(2):
            one = jnp.where(lax.rem(m_lane, 16) == n_first + n, mine, 0.0)
            energy_ref[part, :, n : n + 1] = jnp.sum(one, axis=1, keepdims=True)

    wait_bytes(fwd_send.at[pl.ds(0, NDEV - 1)], fwd_sems.at[0])
    wait_bytes(pot_recv.at[pl.ds(0, NPX - 1)], pot_sems.at[0])
    wait_bytes(ca_send.at[pl.ds(0, NPY - 1)], ca_sems.at[0])
    wait_bytes(cb_send.at[pl.ds(0, NPX - 1)], cb_sems.at[0])
    wait_bytes(back_send.at[pl.ds(0, NDEV - 1)], back_sems.at[0])
    wait_bytes(en_recv.at[pl.ds(0, NDEV - 1)], en_sems.at[0])


def body(waves, col_map, potential, projectors, coupling):
    vmem = pltpu.VMEM
    anywhere = pl.BlockSpec(memory_space=pl.ANY)
    inside = pl.BlockSpec(memory_space=pltpu.VMEM)
    mats = jnp.asarray(dft_tables())
    return pl.pallas_call(
        kernel,
        out_shape=(
            jax.ShapeDtypeStruct((2, BW, LOCAL), F32),
            jax.ShapeDtypeStruct((2, 8, 32), F32),
            jax.ShapeDtypeStruct((2, 8, 2), F32),
        ),
        in_specs=[anywhere] * 6,
        out_specs=(inside, inside, inside),
        scratch_shapes=[
            vmem((2, NB, LOCAL), F32),
            vmem((2, NB, LOCAL), F32),
            vmem((NG, 4, 16), F32),
            vmem((NB, 8), F32),
            vmem((4, 256, 256), BF16),
            pltpu.SMEM((NCOLD,), jnp.int32),
            vmem((2, NB, 2 * LOCAL), BF16),
            vmem((2, 2 * NB, LOCAL), BF16),
            vmem((2, NB, NB), BF16),
            vmem((NDEV, 1, NG), F32),
            vmem((NDEV, 1, NG), F32),
            vmem((16, 4, NG), F32),
            vmem((NPX, 4, NG), F32),
            vmem((NPY, 2, 32, NB), F32),
            vmem((NPY, 2, 32, NB), F32),
            vmem((NPX, 8, NG), F32),
            vmem((NPX, 8, NG), F32),
            vmem((NDEV, 1, NG), F32),
            vmem((NDEV, 1, NG), F32),
            vmem((2 * NPX, 1, NG), F32),
            vmem((NDEV, 1, NG), F32),
            vmem((NPY * NG, NG), F32),
            vmem((2 * NG, 8 * NG), F32),
            vmem((2 * NG, 8 * NG), F32),
            vmem((NPY * NG, NG), F32),
            vmem((NB, NG), F32),
            pltpu.SemaphoreType.DMA((7,)),
            pltpu.SemaphoreType.DMA((6,)),
            pltpu.SemaphoreType.DMA((2,)),
            pltpu.SemaphoreType.DMA((2,)),
            pltpu.SemaphoreType.DMA((2,)),
            pltpu.SemaphoreType.DMA((2,)),
            pltpu.SemaphoreType.DMA((2,)),
            pltpu.SemaphoreType.DMA((2,)),
        ],
        compiler_params=pltpu.CompilerParams(
            collective_id=0, has_side_effects=True, vmem_limit_bytes=40 << 20
        ),
        name="hamiltonian",
    )(waves, col_map, potential, projectors, coupling.reshape(NB, 8), mats)


def solution(mesh):
    placed = (
        P(None, None, ("px", "py")),
        P(("px", "py")),
        P(None, "px", "py"),
        P(None, None, ("px", "py")),
        P(),
    )
    return jax.shard_map(
        body,
        mesh=mesh,
        in_specs=placed,
        out_specs=(P(None, None, ("px", "py")), P(None, "px", "py"), P(None, "px", "py")),
        check_vma=False,
    )
```

```python
import math

import jax
import jax.numpy as jnp
import numpy as np
from jax import lax
from jax.experimental import pallas as pl
from jax.experimental.pallas import tpu as pltpu
from jax.sharding import PartitionSpec as P

NG = 128
NB = 256
BW = 16
NCOLD = 4
GCUT = 50
NPX = 32
NPY = 8
NDEV = NPX * NPY
LOCAL = NCOLD * NG
MESH = pl.DeviceIdType.MESH
F32 = jnp.float32
BF16 = jnp.bfloat16


def dft_tables():
    index = np.arange(NG)
    angle = (index[:, None] * index[None, :] % NG) * (2.0 * math.pi / NG)
    return np.stack([np.cos(angle), np.sin(angle)]).astype(np.float32) / np.float32(math.sqrt(NG))


def split(x):
    high = x.astype(BF16)
    return high, (x - high.astype(F32)).astype(BF16)


def product(a, b, transposed=False):
    dims = (((1,), (1 if transposed else 0,)), ((), ()))

    def dot(u, v):
        return lax.dot_general(u, v, dims, preferred_element_type=F32)

    return dot(a[0], b[0]) + (dot(a[0], b[1]) + dot(a[1], b[0]))


def pair(ref, *index):
    return ref[(0, *index)], ref[(1, *index)]


def far_first(digit, half):
    odd = lax.rem(digit, 2)
    return half + (1 - 2 * odd) * lax.div(digit + 1, 2)


def partner_px(k, p):
    z = lax.rem(lax.div(p, 4) + far_first(lax.div(k, 4), 4), 8)
    y_lo = lax.rem(lax.div(p, 2) + 1 + lax.rem(lax.div(k, 2), 2), 2)
    core = lax.rem(p + 1 + lax.rem(k, 2), 2)
    return z * 4 + y_lo * 2 + core


def partner_py(k, q):
    x = lax.rem(lax.div(q, 2) + far_first(lax.div(k, 2), 2), 4)
    y_hi = lax.rem(q + 1 + lax.rem(k, 2), 2)
    return x * 2 + y_hi


def each_other(p, q, visit):
    z = lax.div(p, 4)
    y_lo = lax.rem(lax.div(p, 2), 2)
    core = lax.rem(p, 2)
    near = [(1 - y_lo, 1 - core), (1 - y_lo, core), (y_lo, 1 - core), (y_lo, core)]
    across = [partner_py(jnp.int32(k), q) for k in range(NPY)]

    def level(digit, carry):
        to_z = lax.rem(z + far_first(digit, 4), 8)
        for to_q in across:
            for to_y, to_core in near:
                visit(to_z, to_y, to_core, to_q)
        return carry

    lax.fori_loop(0, 7, level, 0)
    others = [(to_y, to_core, to_q) for to_q in across for to_y, to_core in near]
    for to_y, to_core, to_q in others[:-1]:
        visit(z, to_y, to_core, to_q)


def remote(src, dst, sems, place):
    return pltpu.make_async_remote_copy(
        src_ref=src,
        dst_ref=dst,
        send_sem=sems.at[0],
        recv_sem=sems.at[1],
        device_id=place,
        device_id_type=MESH,
    )


def wait_bytes(ref, sem):
    pltpu.make_async_copy(ref, ref, sem).wait()


def kernel(
    waves_hbm,
    col_hbm,
    pot_hbm,
    beta_hbm,
    coup_hbm,
    mats_hbm,
    hpsi_ref,
    corr_ref,
    energy_ref,
    waves,
    beta,
    pot,
    coup,
    tables,
    mats,
    col,
    phi_s,
    beta_s,
    sym_s,
    fwd_send,
    fwd_recv,
    pot_send,
    pot_recv,
    ca_send,
    ca_recv,
    cb_send,
    cb_recv,
    back_send,
    back_recv,
    en_send,
    en_recv,
    unpack,
    field,
    grid,
    picked,
    ham,
    load_sems,
    own_sems,
    fwd_sems,
    pot_sems,
    ca_sems,
    cb_sems,
    back_sems,
    en_sems,
):
    p = lax.axis_index("px")
    q = lax.axis_index("py")
    z_low = lax.div(p, 2)
    half = lax.rem(p, 2)
    owner = half * NG + q * 16 + z_low
    slot = q * NPX + p

    barrier = pltpu.get_barrier_semaphore()

    def greet(to_z, to_y, to_core, to_q):
        to_p = to_z * 4 + (to_y * 2 + to_core)
        pl.semaphore_signal(barrier, inc=1, device_id=(to_p, to_q), device_id_type=MESH)

    loads = [
        (waves_hbm.at[:, pl.ds(0, BW)], waves.at[:, pl.ds(0, BW)]),
        (mats_hbm, tables),
        (col_hbm, col),
        (beta_hbm, beta),
        (waves_hbm.at[:, pl.ds(BW, NB - BW)], waves.at[:, pl.ds(BW, NB - BW)]),
        (pot_hbm, pot),
        (coup_hbm, coup),
    ]
    loads = [pltpu.make_async_copy(s, d, load_sems.at[i]) for i, (s, d) in enumerate(loads)]
    for load in loads:
        load.start()
    each_other(p, q, greet)

    lane = lax.broadcasted_iota(jnp.int32, (1, NG), 1)

    loads[0].wait()
    loads[1].wait()
    loads[2].wait()
    z_freq = jnp.where(lane < NG // 2, lane, lane - NG)
    spheres = []
    kinetics = []
    cols = jnp.zeros((1, NG), F32)
    for j in range(NCOLD):
        place = col[j]
        cols = jnp.where(lane == 96 + j, place.astype(F32), cols)
        x = p + NPX * lax.div(place, 16)
        y = q + NPY * lax.rem(place, 16)
        fx = jnp.where(x < NG // 2, x, x - NG)
        fy = jnp.where(y < NG // 2, y, y - NG)
        square = fx * fx + fy * fy + z_freq * z_freq
        spheres.append(jnp.where(square <= GCUT * GCUT, 1.0, 0.0).astype(F32))
        kinetics.append(square.astype(F32) * (2.0 / (NG * NG)))
    sphere = jnp.concatenate(spheres, axis=1)
    kinetic = jnp.concatenate(kinetics, axis=1)

    cosine = tables[0]
    sine = tables[1]
    for i, lower in enumerate((sine, -sine)):
        table = jnp.concatenate(
            [
                jnp.concatenate([cosine, -lower], axis=1),
                jnp.concatenate([lower, cosine], axis=1),
            ]
        )
        high, low = split(table)
        mats[2 * i] = high
        mats[2 * i + 1] = low

    psi_re = waves[0, 0:BW, :] * sphere
    psi_im = waves[1, 0:BW, :] * sphere
    rows = []
    for h in range(2):
        for part in range(2):
            for j in range(NCOLD):
                re = psi_re[h * 8 : h * 8 + 8, j * NG : j * NG + NG]
                im = psi_im[h * 8 : h * 8 + 8, j * NG : j * NG + NG]
                rows.append(jnp.concatenate([re, -im] if part == 0 else [im, re], axis=1))
    z_rows = product(pair(mats.at[pl.ds(2, 2)], slice(0, NG)), split(jnp.concatenate(rows)), True)

    loads[3].wait()
    for part in range(2):
        high, low = split(beta[part] * sphere)
        beta_s[0, part * NB : part * NB + NB, :] = high
        beta_s[1, part * NB : part * NB + NB, :] = low
    zeros = jnp.zeros((32, LOCAL), F32)
    with_re = split(jnp.concatenate([zeros, zeros, psi_re, psi_im, zeros]))
    with_im = split(jnp.concatenate([zeros, zeros, psi_im, -psi_re, zeros]))
    partial = product(pair(beta_s, slice(0, NB)), with_re, True) + product(
        pair(beta_s, slice(NB, 2 * NB)), with_im, True
    )
    for h in range(2):
        part = pltpu.roll(z_rows, 64, 1) if h else z_rows
        rows = jnp.where(lane < 64, part, partial[h * NG : h * NG + NG]) + cols
        fwd_send[h * NG : h * NG + NG, 0, :] = rows

    loads[5].wait()
    for y in range(4):
        pot_send[:, y, :] = pot[y]

    pl.semaphore_wait(barrier, NDEV - 1)

    def send_forward(to_z, to_y, to_core, to_q):
        to_p = to_z * 4 + (to_y * 2 + to_core)
        row = to_z * 2 + (to_core * NG + to_q * 16 + to_y)
        remote(fwd_send.at[row], fwd_recv.at[slot], fwd_sems, (to_p, to_q)).start()

    each_other(p, q, send_forward)
    own_forward = pltpu.make_async_copy(fwd_send.at[owner], fwd_recv.at[slot], own_sems.at[0])
    own_forward.start()

    def send_potential(k, carry):
        to_p = partner_px(k, p)
        remote(pot_send.at[lax.div(to_p, 2)], pot_recv.at[p], pot_sems, (to_p, q)).start()
        return carry

    lax.fori_loop(0, NPX - 1, send_potential, 0)
    own_pot = pltpu.make_async_copy(pot_send.at[z_low], pot_recv.at[p], own_sems.at[1])
    own_pot.start()

    loads[4].wait()
    for part in range(2):
        high, low = split(waves[part] * sphere)
        phi_s[0, :, part * LOCAL : part * LOCAL + LOCAL] = high
        phi_s[1, :, part * LOCAL : part * LOCAL + LOCAL] = low
    phi = pair(phi_s)
    turned = tuple(jnp.concatenate([-x[:, LOCAL:], x[:, :LOCAL]], axis=1) for x in phi)
    ca_send[:, 0] = product(phi, phi, True).reshape(NPY, 32, NB)
    ca_send[:, 1] = product(phi, turned, True).reshape(NPY, 32, NB)

    def send_corr_a(k, carry):
        to_q = partner_py(k, q)
        remote(ca_send.at[to_q], ca_recv.at[q], ca_sems, (p, to_q)).start()
        return carry

    lax.fori_loop(0, NPY - 1, send_corr_a, 0)
    own_ca = pltpu.make_async_copy(ca_send.at[q], ca_recv.at[q], own_sems.at[2])
    own_ca.start()

    loads[6].wait()
    pick_row = lax.broadcasted_iota(jnp.int32, (32, NB), 0)
    pick_lane = lax.broadcasted_iota(jnp.int32, (32, NB), 1)
    pick = jnp.where(lax.div(pick_lane, 8) == pick_row, 1.0, 0.0).astype(F32)
    wide = jnp.dot(
        coup[...].reshape(64, 32), pick, precision=lax.Precision.HIGHEST, preferred_element_type=F32
    )
    blk_j = lax.broadcasted_iota(jnp.int32, (8, 8, NB), 1)
    blk_lane = lax.broadcasted_iota(jnp.int32, (8, 8, NB), 2)
    wide = jnp.where(lax.rem(blk_lane, 8) == blk_j, wide.reshape(8, 8, NB), 0.0)
    wide = jnp.concatenate([jnp.sum(wide, axis=1)] * 32)
    sym_row = lax.broadcasted_iota(jnp.int32, (NB, NB), 0)
    sym_lane = lax.broadcasted_iota(jnp.int32, (NB, NB), 1)
    wide = jnp.where(lax.div(sym_row, 8) == lax.div(sym_lane, 8), wide, 0.0)
    high, low = split(0.5 * (wide + wide.T))
    sym_s[0] = high
    sym_s[1] = low
    picked[...] = jnp.zeros((NPY * NG, NG), F32)

    own_forward.wait()
    wait_bytes(fwd_recv.at[pl.ds(0, NDEV - 1)], fwd_sems.at[1])
    proj_sum = jnp.zeros((NPX, NG), F32)
    for s in range(NPY):
        block = fwd_recv[s * NPX : s * NPX + NPX, 0, :]
        proj_sum = proj_sum + block
        unpack[s * NG : s * NG + NG, :] = jnp.concatenate([block] * 4).T
    proj_sum = jnp.sum(proj_sum, axis=0, keepdims=True)
    proj_row = jnp.where((lane >= 64) & (lane < 96), proj_sum, 0.0)
    x_slot = lax.div(lane, 32).astype(F32) * 16.0
    y_slot = lax.broadcasted_iota(jnp.int32, (16, NPY, NG), 0).astype(F32)
    found = []
    for j in range(NCOLD):
        place = unpack[pl.ds(96 + j, NPY, stride=NG), :] - x_slot
        found.append(y_slot == place[None])
    for b in range(8):
        for part in range(2):
            plane = jnp.zeros((16, NPY, NG), F32)
            for j in range(NCOLD):
                value = unpack[pl.ds(part * 32 + j * 8 + b, NPY, stride=NG), :]
                plane = jnp.where(found[j], value[None], plane)
            field[part * NG : part * NG + NG, b * NG : b * NG + NG] = plane.reshape(NG, NG)

    own_pot.wait()
    wait_bytes(pot_recv.at[pl.ds(0, NPX - 1)], pot_sems.at[1])
    potential = pot_recv[...].reshape(NG, NG)
    potential = jnp.concatenate([potential, potential], axis=1)
    mat_a = pair(mats.at[pl.ds(0, 2)])
    mat_b = pair(mats.at[pl.ds(2, 2)])
    for c in range(4):
        two = slice(c * 256, c * 256 + 256)
        lines = product(mat_a, split(field[:, two]))
        planes = []
        for b in range(2):
            part = lines[:, b * NG : b * NG + NG]
            planes.append(jnp.concatenate([part[:NG], part[NG:]], axis=1))
        real = product(split(jnp.concatenate(planes)), mat_b)
        real = real * jnp.concatenate([potential, potential])
        back = product(split(real), mat_a)
        columns = []
        for b in range(2):
            part = back[b * NG : b * NG + NG]
            columns.append(jnp.concatenate([part[:, :NG], part[:, NG:]]))
        grid[:, two] = product(mat_b, split(jnp.concatenate(columns, axis=1)))
    for b in range(8):
        for part in range(2):
            plane = grid[part * NG : part * NG + NG, b * NG : b * NG + NG].reshape(16, NPY, NG)
            for j in range(NCOLD):
                value = jnp.sum(jnp.where(found[j], plane, 0.0), axis=0)
                picked[pl.ds(part * 32 + j * 8 + b, NPY, stride=NG), :] = value
    for s in range(NPY):
        turned = picked[s * NG : s * NG + NG, :].T
        block = turned[0:32] + turned[32:64] + turned[64:96] + turned[96:128]
        back_send[s * NPX : s * NPX + NPX, 0, :] = block + proj_row

    def send_back(to_z, to_y, to_core, to_q):
        to_p = to_z * 4 + (to_y * 2 + to_core)
        row = to_z * 4 + (to_q * NPX + to_y * 2 + to_core)
        remote(back_send.at[row], back_recv.at[owner], back_sems, (to_p, to_q)).start()

    each_other(p, q, send_back)
    own_back = pltpu.make_async_copy(back_send.at[slot], back_recv.at[owner], own_sems.at[3])
    own_back.start()

    own_ca.wait()
    wait_bytes(ca_recv.at[pl.ds(0, NPY - 1)], ca_sems.at[1])
    total = ca_recv[0]
    for s in range(1, NPY):
        total = total + ca_recv[s]
    total = total.reshape(64, NB)
    total = jnp.concatenate([total, jnp.zeros((64, NB), F32)])
    cb_send[...] = total.T.reshape(NPX, 8, NG)

    def send_corr_b(k, carry):
        to_p = partner_px(k, p)
        remote(cb_send.at[to_p], cb_recv.at[p], cb_sems, (to_p, q)).start()
        return carry

    lax.fori_loop(0, NPX - 1, send_corr_b, 0)
    own_cb = pltpu.make_async_copy(cb_send.at[p], cb_recv.at[p], own_sems.at[4])
    own_cb.start()

    own_back.wait()
    wait_bytes(back_recv.at[pl.ds(0, NDEV - 1)], back_sems.at[1])
    low_rows = back_recv[0:NG, 0, :]
    high_rows = back_recv[NG : 2 * NG, 0, :]
    lines = jnp.where(lane < 64, low_rows, pltpu.roll(high_rows, 64, 1)).T
    lines = product(split(lines), pair(mats.at[pl.ds(2, 2)], slice(0, NG)))
    local_re = []
    local_im = []
    for h in range(2):
        res = [lines[h * 64 + j * 8 : h * 64 + j * 8 + 8] for j in range(4)]
        ims = [lines[h * 64 + 32 + j * 8 : h * 64 + 40 + j * 8] for j in range(4)]
        local_re.append(
            jnp.concatenate([r[:, :NG] + i[:, NG:] for r, i in zip(res, ims)], axis=1)
        )
        local_im.append(
            jnp.concatenate([i[:, :NG] - r[:, NG:] for r, i in zip(res, ims)], axis=1)
        )

    proj = jnp.concatenate([low_rows, high_rows])
    proj = pltpu.roll(proj, 64, 1).T[0:32]
    coef = product(split(proj), pair(sym_s))
    coef_re = coef[0:16]
    coef_im = coef[16:32]
    coef = jnp.concatenate(
        [
            jnp.concatenate([coef_re, -coef_im], axis=1),
            jnp.concatenate([coef_im, coef_re], axis=1),
        ]
    )
    nonlocal_part = product(split(coef), pair(beta_s))
    psi_re = waves[0, 0:BW, :] * sphere
    psi_im = waves[1, 0:BW, :] * sphere
    hpsi_re = kinetic * psi_re + sphere * jnp.concatenate(local_re) + nonlocal_part[0:16]
    hpsi_im = kinetic * psi_im + sphere * jnp.concatenate(local_im) + nonlocal_part[16:32]
    hpsi_ref[0] = hpsi_re
    hpsi_ref[1] = hpsi_im

    rows = []
    for h in range(2):
        re = hpsi_re[h * 8 : h * 8 + 8]
        im = hpsi_im[h * 8 : h * 8 + 8]
        rows.append(jnp.concatenate([re, im], axis=1))
        rows.append(jnp.concatenate([im, -re], axis=1))
    rows = split(jnp.concatenate(rows))
    rows = tuple(jnp.concatenate([x[0:16]] * 8 + [x[16:32]] * 8) for x in rows)
    partial = product(pair(phi_s), rows, True)
    for h in range(2):
        ham[...] = partial[:, h * NG : h * NG + NG]
        block = jnp.zeros((NPX, NG), F32)
        for m in range(8):
            strip = ham[pl.ds(m, NPX, stride=8), :]
            block = jnp.where(lax.div(lane, 16) == m, strip, block)
        en_send[h * NPX : h * NPX + NPX, 0, :] = block

    def send_energy(to_z, to_y, to_core, to_q):
        to_p = to_z * 4 + (to_y * 2 + to_core)
        row = to_z * 4 + (lax.div(to_q, 4) * NPX + to_y * 2 + to_core)
        remote(en_send.at[row], en_recv.at[slot], en_sems, (to_p, to_q)).start()

    each_other(p, q, send_energy)
    own_en = pltpu.make_async_copy(
        en_send.at[lax.div(q, 4) * NPX + p], en_recv.at[slot], own_sems.at[5]
    )
    own_en.start()

    scale = 1.0 / (NDEV * LOCAL)
    own_cb.wait()
    wait_bytes(cb_recv.at[pl.ds(0, NPX - 1)], cb_sems.at[1])
    total = jnp.sum(cb_recv[...], axis=0) * scale
    corr_ref[0] = total[:, 0:32]
    corr_ref[1] = total[:, 32:64]

    own_en.wait()
    wait_bytes(en_recv.at[pl.ds(0, NDEV - 1)], en_sems.at[1])
    total = jnp.zeros((NPX, NG), F32)
    for s in range(NPY):
        total = total + en_recv[s * NPX : s * NPX + NPX, 0, :]
    total = jnp.sum(total, axis=0, keepdims=True) * scale
    m_row = lax.broadcasted_iota(jnp.int32, (8, NG), 0)
    m_lane = lax.broadcasted_iota(jnp.int32, (8, NG), 1)
    mine = jnp.where(lax.div(m_lane, 16) == m_row, total, 0.0)
    for part in range(2):
        n_first = part * 8 + lax.rem(q, 4) * 2
        for n in range(2):
            one = jnp.where(lax.rem(m_lane, 16) == n_first + n, mine, 0.0)
            energy_ref[part, n : n + 1, :] = jnp.sum(one, axis=1)[None]

    wait_bytes(fwd_send.at[pl.ds(0, NDEV - 1)], fwd_sems.at[0])
    wait_bytes(pot_recv.at[pl.ds(0, NPX - 1)], pot_sems.at[0])
    wait_bytes(ca_send.at[pl.ds(0, NPY - 1)], ca_sems.at[0])
    wait_bytes(cb_send.at[pl.ds(0, NPX - 1)], cb_sems.at[0])
    wait_bytes(back_send.at[pl.ds(0, NDEV - 1)], back_sems.at[0])
    wait_bytes(en_recv.at[pl.ds(0, NDEV - 1)], en_sems.at[0])


def body(waves, col_map, potential, projectors, coupling):
    vmem = pltpu.VMEM
    outside = pl.BlockSpec(memory_space=pltpu.HBM)
    inside = pl.BlockSpec(memory_space=pltpu.VMEM)
    mats = jnp.asarray(dft_tables())
    hpsi, corr, energy = pl.pallas_call(
        kernel,
        out_shape=(
            jax.ShapeDtypeStruct((2, BW, LOCAL), F32),
            jax.ShapeDtypeStruct((2, 8, 32), F32),
            jax.ShapeDtypeStruct((2, 2, 8), F32),
        ),
        in_specs=[outside] * 6,
        out_specs=(inside, inside, inside),
        scratch_shapes=[
            vmem((2, NB, LOCAL), F32),
            vmem((2, NB, LOCAL), F32),
            vmem((4, 16, NG), F32),
            vmem((8, 8, 32), F32),
            vmem((2, NG, NG), F32),
            vmem((4, 256, 256), BF16),
            pltpu.SMEM((NCOLD,), jnp.int32),
            vmem((2, NB, 2 * LOCAL), BF16),
            vmem((2, 2 * NB, LOCAL), BF16),
            vmem((2, NB, NB), BF16),
            vmem((NDEV, 1, NG), F32),
            vmem((NDEV, 1, NG), F32),
            vmem((16, 4, NG), F32),
            vmem((NPX, 4, NG), F32),
            vmem((NPY, 2, 32, NB), F32),
            vmem((NPY, 2, 32, NB), F32),
            vmem((NPX, 8, NG), F32),
            vmem((NPX, 8, NG), F32),
            vmem((NDEV, 1, NG), F32),
            vmem((NDEV, 1, NG), F32),
            vmem((2 * NPX, 1, NG), F32),
            vmem((NDEV, 1, NG), F32),
            vmem((NPY * NG, NG), F32),
            vmem((2 * NG, 8 * NG), F32),
            vmem((2 * NG, 8 * NG), F32),
            vmem((NPY * NG, NG), F32),
            vmem((NB, NG), F32),
            pltpu.SemaphoreType.DMA((7,)),
            pltpu.SemaphoreType.DMA((6,)),
            pltpu.SemaphoreType.DMA((2,)),
            pltpu.SemaphoreType.DMA((2,)),
            pltpu.SemaphoreType.DMA((2,)),
            pltpu.SemaphoreType.DMA((2,)),
            pltpu.SemaphoreType.DMA((2,)),
            pltpu.SemaphoreType.DMA((2,)),
        ],
        compiler_params=pltpu.CompilerParams(
            collective_id=0, has_side_effects=True, vmem_limit_bytes=60 << 20
        ),
        name="hamiltonian",
    )(
        waves,
        col_map,
        jnp.transpose(potential, (1, 2, 0)),
        projectors,
        jnp.transpose(coupling, (1, 2, 0)),
        mats,
    )
    return hpsi, corr, jnp.transpose(energy, (0, 2, 1))


def solution(mesh):
    placed = (
        P(None, None, ("px", "py")),
        P(("px", "py")),
        P(None, "px", "py"),
        P(None, None, ("px", "py")),
        P(),
    )
    return jax.shard_map(
        body,
        mesh=mesh,
        in_specs=placed,
        out_specs=(P(None, None, ("px", "py")), P(None, "px", "py"), P(None, "px", "py")),
        check_vma=False,
    )
```

```python
import math

import jax
import jax.numpy as jnp
import numpy as np
from jax import lax
from jax.experimental import pallas as pl
from jax.experimental.pallas import tpu as pltpu
from jax.sharding import PartitionSpec as P

NG = 128
NB = 256
BW = 16
NCOLD = 4
GCUT = 50
NPX = 32
NPY = 8
NDEV = NPX * NPY
LOCAL = NCOLD * NG
MESH = pl.DeviceIdType.MESH
F32 = jnp.float32
BF16 = jnp.bfloat16


def dft_tables():
    index = np.arange(NG)
    angle = (index[:, None] * index[None, :] % NG) * (2.0 * math.pi / NG)
    return np.stack([np.cos(angle), np.sin(angle)]).astype(np.float32) / np.float32(math.sqrt(NG))


def split(x):
    high = x.astype(BF16)
    return high, (x - high.astype(F32)).astype(BF16)


def product(a, b, transposed=False):
    left = jnp.concatenate([a[0], a[0], a[1]], axis=1)
    right = jnp.concatenate([b[0], b[1], b[0]], axis=1 if transposed else 0)
    dims = (((1,), (1 if transposed else 0,)), ((), ()))
    return lax.dot_general(left, right, dims, preferred_element_type=F32)


def pair(ref, *index):
    return ref[(0, *index)], ref[(1, *index)]


def store(ref, row, parts):
    for i, part in enumerate(parts):
        ref[i, row : row + part.shape[0], :] = part


def far_first(digit, half):
    odd = lax.rem(digit, 2)
    return half + (1 - 2 * odd) * lax.div(digit + 1, 2)


def partner_px(k, p):
    z = lax.rem(lax.div(p, 4) + far_first(lax.div(k, 4), 4), 8)
    y_lo = lax.rem(lax.div(p, 2) + 1 + lax.rem(lax.div(k, 2), 2), 2)
    core = lax.rem(p + 1 + lax.rem(k, 2), 2)
    return z * 4 + y_lo * 2 + core


def partner_py(k, q):
    x = lax.rem(lax.div(q, 2) + far_first(lax.div(k, 2), 2), 4)
    y_hi = lax.rem(q + 1 + lax.rem(k, 2), 2)
    return x * 2 + y_hi


def each_other(p, q, visit):
    z = lax.div(p, 4)
    y_lo = lax.rem(lax.div(p, 2), 2)
    core = lax.rem(p, 2)
    near = [(1 - y_lo, 1 - core), (1 - y_lo, core), (y_lo, 1 - core), (y_lo, core)]
    across = [partner_py(jnp.int32(k), q) for k in range(NPY)]

    def level(digit, carry):
        to_z = lax.rem(z + far_first(digit, 4), 8)
        for to_q in across:
            for to_y, to_core in near:
                visit(to_z, to_y, to_core, to_q)
        return carry

    lax.fori_loop(0, 7, level, 0)
    others = [(to_y, to_core, to_q) for to_q in across for to_y, to_core in near]
    for to_y, to_core, to_q in others[:-1]:
        visit(z, to_y, to_core, to_q)


def remote(src, dst, sems, place):
    return pltpu.make_async_remote_copy(
        src_ref=src,
        dst_ref=dst,
        send_sem=sems.at[0],
        recv_sem=sems.at[1],
        device_id=place,
        device_id_type=MESH,
    )


def wait_bytes(ref, sem):
    pltpu.make_async_copy(ref, ref, sem).wait()


def kernel(
    waves_hbm,
    col_hbm,
    pot_hbm,
    beta_hbm,
    coup_hbm,
    mats_hbm,
    hpsi_ref,
    corr_ref,
    energy_ref,
    waves,
    beta,
    pot,
    coup,
    tables,
    mats,
    col,
    phi_s,
    beta_s,
    mixed_s,
    fwd_send,
    fwd_recv,
    pot_send,
    pot_recv,
    ca_send,
    ca_recv,
    cb_send,
    cb_recv,
    back_send,
    back_recv,
    en_send,
    en_recv,
    unpack,
    field,
    grid,
    picked,
    ham,
    lines_s,
    real_s,
    load_sems,
    own_sems,
    fwd_sems,
    pot_sems,
    ca_sems,
    cb_sems,
    back_sems,
    en_sems,
):
    p = lax.axis_index("px")
    q = lax.axis_index("py")
    z_low = lax.div(p, 2)
    half = lax.rem(p, 2)
    owner = half * NG + q * 16 + z_low
    slot = q * NPX + p

    barrier = pltpu.get_barrier_semaphore()

    def greet(to_z, to_y, to_core, to_q):
        to_p = to_z * 4 + (to_y * 2 + to_core)
        pl.semaphore_signal(barrier, inc=1, device_id=(to_p, to_q), device_id_type=MESH)

    loads = [
        (waves_hbm.at[:, pl.ds(0, BW)], waves.at[:, pl.ds(0, BW)]),
        (mats_hbm, tables),
        (col_hbm, col),
        (beta_hbm, beta),
        (waves_hbm.at[:, pl.ds(BW, NB - BW)], waves.at[:, pl.ds(BW, NB - BW)]),
        (pot_hbm, pot),
        (coup_hbm, coup),
    ]
    loads = [pltpu.make_async_copy(s, d, load_sems.at[i]) for i, (s, d) in enumerate(loads)]
    for load in loads:
        load.start()
    each_other(p, q, greet)

    lane = lax.broadcasted_iota(jnp.int32, (1, NG), 1)

    loads[0].wait()
    loads[1].wait()
    loads[2].wait()
    z_freq = jnp.where(lane < NG // 2, lane, lane - NG)
    spheres = []
    kinetics = []
    cols = jnp.zeros((1, NG), F32)
    for j in range(NCOLD):
        place = col[j]
        cols = jnp.where(lane == 96 + j, place.astype(F32), cols)
        x = p + NPX * lax.div(place, 16)
        y = q + NPY * lax.rem(place, 16)
        fx = jnp.where(x < NG // 2, x, x - NG)
        fy = jnp.where(y < NG // 2, y, y - NG)
        square = fx * fx + fy * fy + z_freq * z_freq
        spheres.append(jnp.where(square <= GCUT * GCUT, 1.0, 0.0).astype(F32))
        kinetics.append(square.astype(F32) * (2.0 / (NG * NG)))
    sphere = jnp.concatenate(spheres, axis=1)
    kinetic = jnp.concatenate(kinetics, axis=1)

    cosine = tables[0]
    sine = tables[1]
    for i, lower in enumerate((sine, -sine)):
        table = jnp.concatenate(
            [
                jnp.concatenate([cosine, -lower], axis=1),
                jnp.concatenate([lower, cosine], axis=1),
            ]
        )
        high, low = split(table)
        mats[2 * i] = high
        mats[2 * i + 1] = low

    psi_re = waves[0, 0:BW, :] * sphere
    psi_im = waves[1, 0:BW, :] * sphere
    rows = []
    for h in range(2):
        for part in range(2):
            for j in range(NCOLD):
                re = psi_re[h * 8 : h * 8 + 8, j * NG : j * NG + NG]
                im = psi_im[h * 8 : h * 8 + 8, j * NG : j * NG + NG]
                rows.append(jnp.concatenate([re, -im] if part == 0 else [im, re], axis=1))
    z_rows = product(pair(mats.at[pl.ds(2, 2)], slice(0, NG)), split(jnp.concatenate(rows)), True)

    loads[3].wait()
    for part in range(2):
        high, low = split(beta[part] * sphere)
        beta_s[0, part * NB : part * NB + NB, :] = high
        beta_s[1, part * NB : part * NB + NB, :] = low
    zeros = jnp.zeros((32, LOCAL), F32)
    with_re = split(jnp.concatenate([zeros, zeros, psi_re, psi_im, zeros]))
    with_im = split(jnp.concatenate([zeros, zeros, psi_im, -psi_re, zeros]))
    partial = product(pair(beta_s, slice(0, NB)), with_re, True) + product(
        pair(beta_s, slice(NB, 2 * NB)), with_im, True
    )
    for h in range(2):
        part = pltpu.roll(z_rows, 64, 1) if h else z_rows
        rows = jnp.where(lane < 64, part, partial[h * NG : h * NG + NG]) + cols
        fwd_send[h * NG : h * NG + NG, 0, :] = rows

    loads[5].wait()
    for y in range(4):
        pot_send[:, y, :] = pot[y]

    pl.semaphore_wait(barrier, NDEV - 1)

    def send_forward(to_z, to_y, to_core, to_q):
        to_p = to_z * 4 + (to_y * 2 + to_core)
        row = to_z * 2 + (to_core * NG + to_q * 16 + to_y)
        remote(fwd_send.at[row], fwd_recv.at[slot], fwd_sems, (to_p, to_q)).start()

    each_other(p, q, send_forward)
    own_forward = pltpu.make_async_copy(fwd_send.at[owner], fwd_recv.at[slot], own_sems.at[0])
    own_forward.start()

    def send_potential(k, carry):
        to_p = partner_px(k, p)
        remote(pot_send.at[lax.div(to_p, 2)], pot_recv.at[p], pot_sems, (to_p, q)).start()
        return carry

    lax.fori_loop(0, NPX - 1, send_potential, 0)
    own_pot = pltpu.make_async_copy(pot_send.at[z_low], pot_recv.at[p], own_sems.at[1])
    own_pot.start()

    loads[4].wait()
    for part in range(2):
        high, low = split(waves[part] * sphere)
        phi_s[0, :, part * LOCAL : part * LOCAL + LOCAL] = high
        phi_s[1, :, part * LOCAL : part * LOCAL + LOCAL] = low
    phi = pair(phi_s)
    turned = tuple(jnp.concatenate([-x[:, LOCAL:], x[:, :LOCAL]], axis=1) for x in phi)
    ca_send[:, 0] = product(phi, phi, True).reshape(NPY, 32, NB)
    ca_send[:, 1] = product(phi, turned, True).reshape(NPY, 32, NB)

    def send_corr_a(k, carry):
        to_q = partner_py(k, q)
        remote(ca_send.at[to_q], ca_recv.at[q], ca_sems, (p, to_q)).start()
        return carry

    lax.fori_loop(0, NPY - 1, send_corr_a, 0)
    own_ca = pltpu.make_async_copy(ca_send.at[q], ca_recv.at[q], own_sems.at[2])
    own_ca.start()

    loads[6].wait()
    pick_row = lax.broadcasted_iota(jnp.int32, (32, NB), 0)
    pick_lane = lax.broadcasted_iota(jnp.int32, (32, NB), 1)
    pick = jnp.where(lax.div(pick_lane, 8) == pick_row, 1.0, 0.0).astype(F32)
    wide = jnp.dot(
        coup[...].reshape(64, 32), pick, precision=lax.Precision.HIGHEST, preferred_element_type=F32
    )
    blk_j = lax.broadcasted_iota(jnp.int32, (8, 8, NB), 1)
    blk_lane = lax.broadcasted_iota(jnp.int32, (8, 8, NB), 2)
    wide = jnp.where(lax.rem(blk_lane, 8) == blk_j, wide.reshape(8, 8, NB), 0.0)
    wide = jnp.concatenate([jnp.sum(wide, axis=1)] * 32)
    sym_row = lax.broadcasted_iota(jnp.int32, (NB, NB), 0)
    sym_lane = lax.broadcasted_iota(jnp.int32, (NB, NB), 1)
    wide = jnp.where(lax.div(sym_row, 8) == lax.div(sym_lane, 8), wide, 0.0)
    high, low = split(0.5 * (wide + wide.T))
    for part in range(2):
        rows = slice(part * NB, part * NB + NB)
        store(mixed_s, part * NB, split(product((high, low), pair(beta_s, rows))))
    picked[...] = jnp.zeros((NPY * NG, NG), F32)

    own_forward.wait()
    wait_bytes(fwd_recv.at[pl.ds(0, NDEV - 1)], fwd_sems.at[1])
    proj_sum = jnp.zeros((NPX, NG), F32)
    for s in range(NPY):
        block = fwd_recv[s * NPX : s * NPX + NPX, 0, :]
        proj_sum = proj_sum + block
        unpack[s * NG : s * NG + NG, :] = jnp.concatenate([block] * 4).T
    proj_sum = jnp.sum(proj_sum, axis=0, keepdims=True)
    proj_row = jnp.where((lane >= 64) & (lane < 96), proj_sum, 0.0)
    x_slot = lax.div(lane, 32).astype(F32) * 16.0
    y_slot = lax.broadcasted_iota(jnp.int32, (16, NPY, NG), 0).astype(F32)
    found = []
    for j in range(NCOLD):
        place = unpack[pl.ds(96 + j, NPY, stride=NG), :] - x_slot
        found.append(y_slot == place[None])
    for b in range(8):
        for part in range(2):
            plane = jnp.zeros((16, NPY, NG), F32)
            for j in range(NCOLD):
                value = unpack[pl.ds(part * 32 + j * 8 + b, NPY, stride=NG), :]
                plane = jnp.where(found[j], value[None], plane)
            field[part * NG : part * NG + NG, b * NG : b * NG + NG] = plane.reshape(NG, NG)

    own_pot.wait()
    wait_bytes(pot_recv.at[pl.ds(0, NPX - 1)], pot_sems.at[1])
    potential = pot_recv[...].reshape(NG, NG)
    potential = jnp.concatenate([potential, potential], axis=1)
    potential = jnp.concatenate([potential, potential])
    mat_a = pair(mats.at[pl.ds(0, 2)])
    mat_b = pair(mats.at[pl.ds(2, 2)])
    for c in range(4):
        two = slice(c * 256, c * 256 + 256)
        lines = product(mat_a, split(field[:, two]))
        for b in range(2):
            part = lines[:, b * NG : b * NG + NG]
            row = (2 * c + b) * NG
            store(lines_s, row, split(jnp.concatenate([part[:NG], part[NG:]], axis=1)))
    for c in range(4):
        two = slice(c * 256, c * 256 + 256)
        real = product(pair(lines_s, two), mat_b) * potential
        store(real_s, c * 256, split(real))
    for c in range(4):
        two = slice(c * 256, c * 256 + 256)
        back = product(pair(real_s, two), mat_a)
        columns = []
        for b in range(2):
            part = back[b * NG : b * NG + NG]
            columns.append(jnp.concatenate([part[:, :NG], part[:, NG:]]))
        store(lines_s, c * 256, split(jnp.concatenate(columns, axis=1)))
    for c in range(4):
        two = slice(c * 256, c * 256 + 256)
        grid[:, two] = product(mat_b, pair(lines_s, two))
    for b in range(8):
        for part in range(2):
            plane = grid[part * NG : part * NG + NG, b * NG : b * NG + NG].reshape(16, NPY, NG)
            for j in range(NCOLD):
                value = jnp.sum(jnp.where(found[j], plane, 0.0), axis=0)
                picked[pl.ds(part * 32 + j * 8 + b, NPY, stride=NG), :] = value
    for s in range(NPY):
        turned = picked[s * NG : s * NG + NG, :].T
        block = turned[0:32] + turned[32:64] + turned[64:96] + turned[96:128]
        back_send[s * NPX : s * NPX + NPX, 0, :] = block + proj_row

    def send_back(to_z, to_y, to_core, to_q):
        to_p = to_z * 4 + (to_y * 2 + to_core)
        row = to_z * 4 + (to_q * NPX + to_y * 2 + to_core)
        remote(back_send.at[row], back_recv.at[owner], back_sems, (to_p, to_q)).start()

    each_other(p, q, send_back)
    own_back = pltpu.make_async_copy(back_send.at[slot], back_recv.at[owner], own_sems.at[3])
    own_back.start()

    own_ca.wait()
    wait_bytes(ca_recv.at[pl.ds(0, NPY - 1)], ca_sems.at[1])
    total = ca_recv[0]
    for s in range(1, NPY):
        total = total + ca_recv[s]
    total = total.reshape(64, NB)
    total = jnp.concatenate([total, jnp.zeros((64, NB), F32)])
    cb_send[...] = total.T.reshape(NPX, 8, NG)

    def send_corr_b(k, carry):
        to_p = partner_px(k, p)
        remote(cb_send.at[to_p], cb_recv.at[p], cb_sems, (to_p, q)).start()
        return carry

    lax.fori_loop(0, NPX - 1, send_corr_b, 0)
    own_cb = pltpu.make_async_copy(cb_send.at[p], cb_recv.at[p], own_sems.at[4])
    own_cb.start()

    own_back.wait()
    wait_bytes(back_recv.at[pl.ds(0, NDEV - 1)], back_sems.at[1])
    low_rows = back_recv[0:NG, 0, :]
    high_rows = back_recv[NG : 2 * NG, 0, :]
    lines = jnp.where(lane < 64, low_rows, pltpu.roll(high_rows, 64, 1)).T
    lines = product(split(lines), pair(mats.at[pl.ds(2, 2)], slice(0, NG)))
    local_re = []
    local_im = []
    for h in range(2):
        res = [lines[h * 64 + j * 8 : h * 64 + j * 8 + 8] for j in range(4)]
        ims = [lines[h * 64 + 32 + j * 8 : h * 64 + 40 + j * 8] for j in range(4)]
        local_re.append(
            jnp.concatenate([r[:, :NG] + i[:, NG:] for r, i in zip(res, ims)], axis=1)
        )
        local_im.append(
            jnp.concatenate([i[:, :NG] - r[:, NG:] for r, i in zip(res, ims)], axis=1)
        )

    proj = jnp.concatenate([low_rows, high_rows])
    proj = pltpu.roll(proj, 64, 1).T[0:32]
    proj_re = proj[0:16]
    proj_im = proj[16:32]
    proj = jnp.concatenate(
        [
            jnp.concatenate([proj_re, -proj_im], axis=1),
            jnp.concatenate([proj_im, proj_re], axis=1),
        ]
    )
    nonlocal_part = product(split(proj), pair(mixed_s))
    psi_re = waves[0, 0:BW, :] * sphere
    psi_im = waves[1, 0:BW, :] * sphere
    hpsi_re = kinetic * psi_re + sphere * jnp.concatenate(local_re) + nonlocal_part[0:16]
    hpsi_im = kinetic * psi_im + sphere * jnp.concatenate(local_im) + nonlocal_part[16:32]
    hpsi_ref[0] = hpsi_re
    hpsi_ref[1] = hpsi_im

    rows = []
    for h in range(2):
        re = hpsi_re[h * 8 : h * 8 + 8]
        im = hpsi_im[h * 8 : h * 8 + 8]
        rows.append(jnp.concatenate([re, im], axis=1))
        rows.append(jnp.concatenate([im, -re], axis=1))
    rows = split(jnp.concatenate(rows))
    rows = tuple(jnp.concatenate([x[0:16]] * 8 + [x[16:32]] * 8) for x in rows)
    partial = product(pair(phi_s), rows, True)
    for h in range(2):
        ham[...] = partial[:, h * NG : h * NG + NG]
        block = jnp.zeros((NPX, NG), F32)
        for m in range(8):
            strip = ham[pl.ds(m, NPX, stride=8), :]
            block = jnp.where(lax.div(lane, 16) == m, strip, block)
        en_send[h * NPX : h * NPX + NPX, 0, :] = block

    def send_energy(to_z, to_y, to_core, to_q):
        to_p = to_z * 4 + (to_y * 2 + to_core)
        row = to_z * 4 + (lax.div(to_q, 4) * NPX + to_y * 2 + to_core)
        remote(en_send.at[row], en_recv.at[slot], en_sems, (to_p, to_q)).start()

    each_other(p, q, send_energy)
    own_en = pltpu.make_async_copy(
        en_send.at[lax.div(q, 4) * NPX + p], en_recv.at[slot], own_sems.at[5]
    )
    own_en.start()

    scale = 1.0 / (NDEV * LOCAL)
    own_cb.wait()
    wait_bytes(cb_recv.at[pl.ds(0, NPX - 1)], cb_sems.at[1])
    total = jnp.sum(cb_recv[...], axis=0) * scale
    corr_ref[0] = total[:, 0:32]
    corr_ref[1] = total[:, 32:64]

    own_en.wait()
    wait_bytes(en_recv.at[pl.ds(0, NDEV - 1)], en_sems.at[1])
    total = jnp.zeros((NPX, NG), F32)
    for s in range(NPY):
        total = total + en_recv[s * NPX : s * NPX + NPX, 0, :]
    total = jnp.sum(total, axis=0, keepdims=True) * scale
    m_row = lax.broadcasted_iota(jnp.int32, (8, NG), 0)
    m_lane = lax.broadcasted_iota(jnp.int32, (8, NG), 1)
    mine = jnp.where(lax.div(m_lane, 16) == m_row, total, 0.0)
    for part in range(2):
        n_first = part * 8 + lax.rem(q, 4) * 2
        for n in range(2):
            one = jnp.where(lax.rem(m_lane, 16) == n_first + n, mine, 0.0)
            energy_ref[part, n : n + 1, :] = jnp.sum(one, axis=1)[None]

    wait_bytes(fwd_send.at[pl.ds(0, NDEV - 1)], fwd_sems.at[0])
    wait_bytes(pot_recv.at[pl.ds(0, NPX - 1)], pot_sems.at[0])
    wait_bytes(ca_send.at[pl.ds(0, NPY - 1)], ca_sems.at[0])
    wait_bytes(cb_send.at[pl.ds(0, NPX - 1)], cb_sems.at[0])
    wait_bytes(back_send.at[pl.ds(0, NDEV - 1)], back_sems.at[0])
    wait_bytes(en_recv.at[pl.ds(0, NDEV - 1)], en_sems.at[0])


def finish(hpsi, corr, energy, hpsi_out, corr_out, energy_out, sems):
    pairs = ((hpsi, hpsi_out), (corr, corr_out), (energy, energy_out))
    copies = [pltpu.make_async_copy(a, b, sems.at[i]) for i, (a, b) in enumerate(pairs)]
    for copy in copies:
        copy.start()
    for copy in copies:
        copy.wait()


def body(waves, col_map, potential, projectors, coupling):
    vmem = pltpu.VMEM
    inside = pl.BlockSpec(memory_space=pltpu.VMEM)
    outside = pl.BlockSpec(memory_space=pltpu.HBM)
    mats = jnp.asarray(dft_tables())
    shapes = (
        jax.ShapeDtypeStruct((2, BW, LOCAL), F32),
        jax.ShapeDtypeStruct((2, 8, 32), F32),
        jax.ShapeDtypeStruct((2, 2, 8), F32),
    )
    arrays = (
        waves,
        col_map,
        jnp.transpose(potential, (1, 2, 0)),
        projectors,
        jnp.transpose(coupling, (1, 2, 0)),
        mats,
    )
    results = pl.pallas_call(
        kernel,
        out_shape=tuple(vmem(x.shape, x.dtype) for x in shapes),
        in_specs=[outside] * 6,
        out_specs=(inside, inside, inside),
        scratch_shapes=[
            vmem((2, NB, LOCAL), F32),
            vmem((2, NB, LOCAL), F32),
            vmem((4, 16, NG), F32),
            vmem((8, 8, 32), F32),
            vmem((2, NG, NG), F32),
            vmem((4, 256, 256), BF16),
            pltpu.SMEM((NCOLD,), jnp.int32),
            vmem((2, NB, 2 * LOCAL), BF16),
            vmem((2, 2 * NB, LOCAL), BF16),
            vmem((2, 2 * NB, LOCAL), BF16),
            vmem((NDEV, 1, NG), F32),
            vmem((NDEV, 1, NG), F32),
            vmem((16, 4, NG), F32),
            vmem((NPX, 4, NG), F32),
            vmem((NPY, 2, 32, NB), F32),
            vmem((NPY, 2, 32, NB), F32),
            vmem((NPX, 8, NG), F32),
            vmem((NPX, 8, NG), F32),
            vmem((NDEV, 1, NG), F32),
            vmem((NDEV, 1, NG), F32),
            vmem((2 * NPX, 1, NG), F32),
            vmem((NDEV, 1, NG), F32),
            vmem((NPY * NG, NG), F32),
            vmem((2 * NG, 8 * NG), F32),
            vmem((2 * NG, 8 * NG), F32),
            vmem((NPY * NG, NG), F32),
            vmem((NB, NG), F32),
            vmem((2, 8 * NG, 256), BF16),
            vmem((2, 8 * NG, 256), BF16),
            pltpu.SemaphoreType.DMA((7,)),
            pltpu.SemaphoreType.DMA((6,)),
            pltpu.SemaphoreType.DMA((2,)),
            pltpu.SemaphoreType.DMA((2,)),
            pltpu.SemaphoreType.DMA((2,)),
            pltpu.SemaphoreType.DMA((2,)),
            pltpu.SemaphoreType.DMA((2,)),
            pltpu.SemaphoreType.DMA((2,)),
        ],
        compiler_params=pltpu.CompilerParams(
            collective_id=0, has_side_effects=True, vmem_limit_bytes=40 << 20
        ),
        name="hamiltonian",
    )(*(pltpu.with_memory_space_constraint(x, pltpu.HBM) for x in arrays))
    hpsi, corr, energy = pl.pallas_call(
        finish,
        out_shape=shapes,
        in_specs=[inside] * 3,
        out_specs=(outside, outside, outside),
        scratch_shapes=[pltpu.SemaphoreType.DMA((3,))],
        name="finish",
    )(*(pltpu.with_memory_space_constraint(x, pltpu.VMEM) for x in results))
    return hpsi, corr, jnp.transpose(energy, (0, 2, 1))


def solution(mesh):
    placed = (
        P(None, None, ("px", "py")),
        P(("px", "py")),
        P(None, "px", "py"),
        P(None, None, ("px", "py")),
        P(),
    )
    return jax.shard_map(
        body,
        mesh=mesh,
        in_specs=placed,
        out_specs=(P(None, None, ("px", "py")), P(None, "px", "py"), P(None, "px", "py")),
        check_vma=False,
    )
```

```python
import math

import jax
import jax.numpy as jnp
import numpy as np
from jax import lax
from jax.experimental import pallas as pl
from jax.experimental.pallas import tpu as pltpu
from jax.sharding import PartitionSpec as P

NG = 128
NB = 256
BW = 16
NCOLD = 4
GCUT = 50
NPX = 32
NPY = 8
NDEV = NPX * NPY
LOCAL = NCOLD * NG
MESH = pl.DeviceIdType.MESH
F32 = jnp.float32
BF16 = jnp.bfloat16


def dft_tables():
    index = np.arange(NG)
    angle = (index[:, None] * index[None, :] % NG) * (2.0 * math.pi / NG)
    return np.stack([np.cos(angle), np.sin(angle)]).astype(np.float32) / np.float32(math.sqrt(NG))


def split(x):
    high = x.astype(BF16)
    return high, (x - high.astype(F32)).astype(BF16)


def product(a, b, transposed=False):
    left = jnp.concatenate([a[0], a[0], a[1]], axis=1)
    right = jnp.concatenate([b[0], b[1], b[0]], axis=1 if transposed else 0)
    dims = (((1,), (1 if transposed else 0,)), ((), ()))
    return lax.dot_general(left, right, dims, preferred_element_type=F32)


def pair(ref, *index):
    return ref[(0, *index)], ref[(1, *index)]


def store(ref, row, parts):
    for i, part in enumerate(parts):
        ref[i, row : row + part.shape[0], :] = part


def far_first(digit, half):
    odd = lax.rem(digit, 2)
    return half + (1 - 2 * odd) * lax.div(digit + 1, 2)


def partner_px(k, p):
    z = lax.rem(lax.div(p, 4) + far_first(lax.div(k, 4), 4), 8)
    y_lo = lax.rem(lax.div(p, 2) + 1 + lax.rem(lax.div(k, 2), 2), 2)
    core = lax.rem(p + 1 + lax.rem(k, 2), 2)
    return z * 4 + y_lo * 2 + core


def partner_py(k, q):
    x = lax.rem(lax.div(q, 2) + far_first(lax.div(k, 2), 2), 4)
    y_hi = lax.rem(q + 1 + lax.rem(k, 2), 2)
    return x * 2 + y_hi


def each_other(p, q, visit):
    z = lax.div(p, 4)
    y_lo = lax.rem(lax.div(p, 2), 2)
    core = lax.rem(p, 2)
    x = lax.div(q, 2)
    y_hi = lax.rem(q, 2)
    to_z = [lax.rem(z + d, 8) for d in range(8)]
    to_y = [y_lo, 1 - y_lo]
    to_core = [core, 1 - core]
    to_q = [[lax.rem(x + d, 4) * 2 + h for h in (y_hi, 1 - y_hi)] for d in range(4)]
    hops = []
    for dz, dx, hi, lo, dc in np.ndindex(8, 4, 2, 2, 2):
        far = min(dz, 8 - dz) + min(dx, 4 - dx) + (1 if lo else 2 * hi) + 0.6 * dc
        hops.append((-far, dz, dx, hi, lo, dc))
    for _, dz, dx, hi, lo, dc in sorted(hops)[:-1]:
        visit(to_z[dz], to_y[lo], to_core[dc], to_q[dx][hi])


def remote(src, dst, sems, place):
    return pltpu.make_async_remote_copy(
        src_ref=src,
        dst_ref=dst,
        send_sem=sems.at[0],
        recv_sem=sems.at[1],
        device_id=place,
        device_id_type=MESH,
    )


def wait_bytes(ref, sem):
    pltpu.make_async_copy(ref, ref, sem).wait()


def kernel(
    waves_hbm,
    col_hbm,
    pot_hbm,
    beta_hbm,
    coup_hbm,
    mats_hbm,
    hpsi_ref,
    corr_ref,
    energy_ref,
    waves,
    beta,
    pot,
    coup,
    tables,
    mats,
    col,
    phi_s,
    beta_s,
    mixed_s,
    fwd_send,
    fwd_recv,
    pot_send,
    pot_recv,
    ca_send,
    ca_recv,
    cb_send,
    cb_recv,
    back_send,
    back_recv,
    en_send,
    en_recv,
    unpack,
    field,
    grid,
    picked,
    ham,
    lines_s,
    real_s,
    load_sems,
    own_sems,
    fwd_sems,
    pot_sems,
    ca_sems,
    cb_sems,
    back_sems,
    en_sems,
):
    p = lax.axis_index("px")
    q = lax.axis_index("py")
    z_low = lax.div(p, 2)
    half = lax.rem(p, 2)
    owner = half * NG + q * 16 + z_low
    slot = q * NPX + p

    barrier = pltpu.get_barrier_semaphore()

    def greet(to_z, to_y, to_core, to_q):
        to_p = to_z * 4 + (to_y * 2 + to_core)
        pl.semaphore_signal(barrier, inc=1, device_id=(to_p, to_q), device_id_type=MESH)

    loads = [
        (waves_hbm.at[:, pl.ds(0, BW)], waves.at[:, pl.ds(0, BW)]),
        (mats_hbm, tables),
        (col_hbm, col),
        (beta_hbm, beta),
        (waves_hbm.at[:, pl.ds(BW, NB - BW)], waves.at[:, pl.ds(BW, NB - BW)]),
        (pot_hbm, pot),
        (coup_hbm, coup),
    ]
    loads = [pltpu.make_async_copy(s, d, load_sems.at[i]) for i, (s, d) in enumerate(loads)]
    for load in loads:
        load.start()
    each_other(p, q, greet)

    lane = lax.broadcasted_iota(jnp.int32, (1, NG), 1)

    loads[0].wait()
    loads[1].wait()
    loads[2].wait()
    z_freq = jnp.where(lane < NG // 2, lane, lane - NG)
    spheres = []
    kinetics = []
    cols = jnp.zeros((1, NG), F32)
    for j in range(NCOLD):
        place = col[j]
        cols = jnp.where(lane == 96 + j, place.astype(F32), cols)
        x = p + NPX * lax.div(place, 16)
        y = q + NPY * lax.rem(place, 16)
        fx = jnp.where(x < NG // 2, x, x - NG)
        fy = jnp.where(y < NG // 2, y, y - NG)
        square = fx * fx + fy * fy + z_freq * z_freq
        spheres.append(jnp.where(square <= GCUT * GCUT, 1.0, 0.0).astype(F32))
        kinetics.append(square.astype(F32) * (2.0 / (NG * NG)))
    sphere = jnp.concatenate(spheres, axis=1)
    kinetic = jnp.concatenate(kinetics, axis=1)

    cosine = tables[0]
    sine = tables[1]
    for i, lower in enumerate((sine, -sine)):
        table = jnp.concatenate(
            [
                jnp.concatenate([cosine, -lower], axis=1),
                jnp.concatenate([lower, cosine], axis=1),
            ]
        )
        high, low = split(table)
        mats[2 * i] = high
        mats[2 * i + 1] = low

    psi_re = waves[0, 0:BW, :] * sphere
    psi_im = waves[1, 0:BW, :] * sphere
    rows = []
    for h in range(2):
        for part in range(2):
            for j in range(NCOLD):
                re = psi_re[h * 8 : h * 8 + 8, j * NG : j * NG + NG]
                im = psi_im[h * 8 : h * 8 + 8, j * NG : j * NG + NG]
                rows.append(jnp.concatenate([re, -im] if part == 0 else [im, re], axis=1))
    z_rows = product(pair(mats.at[pl.ds(2, 2)], slice(0, NG)), split(jnp.concatenate(rows)), True)

    loads[3].wait()
    for part in range(2):
        high, low = split(beta[part] * sphere)
        beta_s[0, part * NB : part * NB + NB, :] = high
        beta_s[1, part * NB : part * NB + NB, :] = low
    zeros = jnp.zeros((32, LOCAL), F32)
    with_re = split(jnp.concatenate([zeros, zeros, psi_re, psi_im, zeros]))
    with_im = split(jnp.concatenate([zeros, zeros, psi_im, -psi_re, zeros]))
    partial = product(pair(beta_s, slice(0, NB)), with_re, True) + product(
        pair(beta_s, slice(NB, 2 * NB)), with_im, True
    )
    for h in range(2):
        part = pltpu.roll(z_rows, 64, 1) if h else z_rows
        rows = jnp.where(lane < 64, part, partial[h * NG : h * NG + NG]) + cols
        fwd_send[h * NG : h * NG + NG, 0, :] = rows

    loads[5].wait()
    for y in range(4):
        pot_send[:, y, :] = pot[y]

    pl.semaphore_wait(barrier, NDEV - 1)

    def send_forward(to_z, to_y, to_core, to_q):
        to_p = to_z * 4 + (to_y * 2 + to_core)
        row = to_z * 2 + (to_core * NG + to_q * 16 + to_y)
        remote(fwd_send.at[row], fwd_recv.at[slot], fwd_sems, (to_p, to_q)).start()

    each_other(p, q, send_forward)
    own_forward = pltpu.make_async_copy(fwd_send.at[owner], fwd_recv.at[slot], own_sems.at[0])
    own_forward.start()

    def send_potential(k, carry):
        to_p = partner_px(k, p)
        remote(pot_send.at[lax.div(to_p, 2)], pot_recv.at[p], pot_sems, (to_p, q)).start()
        return carry

    lax.fori_loop(0, NPX - 1, send_potential, 0)
    own_pot = pltpu.make_async_copy(pot_send.at[z_low], pot_recv.at[p], own_sems.at[1])
    own_pot.start()

    loads[4].wait()
    for part in range(2):
        high, low = split(waves[part] * sphere)
        phi_s[0, :, part * LOCAL : part * LOCAL + LOCAL] = high
        phi_s[1, :, part * LOCAL : part * LOCAL + LOCAL] = low
    phi = pair(phi_s)
    turned = tuple(jnp.concatenate([-x[:, LOCAL:], x[:, :LOCAL]], axis=1) for x in phi)
    ca_send[:, 0] = product(phi, phi, True).reshape(NPY, 32, NB)
    ca_send[:, 1] = product(phi, turned, True).reshape(NPY, 32, NB)

    def send_corr_a(k, carry):
        to_q = partner_py(k, q)
        remote(ca_send.at[to_q], ca_recv.at[q], ca_sems, (p, to_q)).start()
        return carry

    lax.fori_loop(0, NPY - 1, send_corr_a, 0)
    own_ca = pltpu.make_async_copy(ca_send.at[q], ca_recv.at[q], own_sems.at[2])
    own_ca.start()

    loads[6].wait()
    pick_row = lax.broadcasted_iota(jnp.int32, (32, NB), 0)
    pick_lane = lax.broadcasted_iota(jnp.int32, (32, NB), 1)
    pick = jnp.where(lax.div(pick_lane, 8) == pick_row, 1.0, 0.0).astype(F32)
    wide = jnp.dot(
        coup[...].reshape(64, 32), pick, precision=lax.Precision.HIGHEST, preferred_element_type=F32
    )
    blk_j = lax.broadcasted_iota(jnp.int32, (8, 8, NB), 1)
    blk_lane = lax.broadcasted_iota(jnp.int32, (8, 8, NB), 2)
    wide = jnp.where(lax.rem(blk_lane, 8) == blk_j, wide.reshape(8, 8, NB), 0.0)
    wide = jnp.concatenate([jnp.sum(wide, axis=1)] * 32)
    sym_row = lax.broadcasted_iota(jnp.int32, (NB, NB), 0)
    sym_lane = lax.broadcasted_iota(jnp.int32, (NB, NB), 1)
    wide = jnp.where(lax.div(sym_row, 8) == lax.div(sym_lane, 8), wide, 0.0)
    high, low = split(0.5 * (wide + wide.T))
    for part in range(2):
        rows = slice(part * NB, part * NB + NB)
        store(mixed_s, part * NB, split(product((high, low), pair(beta_s, rows))))
    picked[...] = jnp.zeros((NPY * NG, NG), F32)

    own_forward.wait()
    wait_bytes(fwd_recv.at[pl.ds(0, NDEV - 1)], fwd_sems.at[1])
    proj_sum = jnp.zeros((NPX, NG), F32)
    for s in range(NPY):
        block = fwd_recv[s * NPX : s * NPX + NPX, 0, :]
        proj_sum = proj_sum + block
        unpack[s * NG : s * NG + NG, :] = jnp.concatenate([block] * 4).T
    proj_sum = jnp.sum(proj_sum, axis=0, keepdims=True)
    proj_row = jnp.where((lane >= 64) & (lane < 96), proj_sum, 0.0)
    x_slot = lax.div(lane, 32).astype(F32) * 16.0
    y_slot = lax.broadcasted_iota(jnp.int32, (16, NPY, NG), 0).astype(F32)
    found = []
    for j in range(NCOLD):
        place = unpack[pl.ds(96 + j, NPY, stride=NG), :] - x_slot
        found.append(y_slot == place[None])
    for b in range(8):
        for part in range(2):
            plane = jnp.zeros((16, NPY, NG), F32)
            for j in range(NCOLD):
                value = unpack[pl.ds(part * 32 + j * 8 + b, NPY, stride=NG), :]
                plane = jnp.where(found[j], value[None], plane)
            field[part * NG : part * NG + NG, b * NG : b * NG + NG] = plane.reshape(NG, NG)

    own_pot.wait()
    wait_bytes(pot_recv.at[pl.ds(0, NPX - 1)], pot_sems.at[1])
    potential = pot_recv[...].reshape(NG, NG)
    potential = jnp.concatenate([potential, potential], axis=1)
    potential = jnp.concatenate([potential, potential])
    mat_a = pair(mats.at[pl.ds(0, 2)])
    mat_b = pair(mats.at[pl.ds(2, 2)])
    for c in range(4):
        two = slice(c * 256, c * 256 + 256)
        lines = product(mat_a, split(field[:, two]))
        for b in range(2):
            part = lines[:, b * NG : b * NG + NG]
            row = (2 * c + b) * NG
            store(lines_s, row, split(jnp.concatenate([part[:NG], part[NG:]], axis=1)))
    for c in range(4):
        two = slice(c * 256, c * 256 + 256)
        real = product(pair(lines_s, two), mat_b) * potential
        store(real_s, c * 256, split(real))
    for c in range(4):
        two = slice(c * 256, c * 256 + 256)
        back = product(pair(real_s, two), mat_a)
        columns = []
        for b in range(2):
            part = back[b * NG : b * NG + NG]
            columns.append(jnp.concatenate([part[:, :NG], part[:, NG:]]))
        store(lines_s, c * 256, split(jnp.concatenate(columns, axis=1)))
    for c in range(4):
        two = slice(c * 256, c * 256 + 256)
        grid[:, two] = product(mat_b, pair(lines_s, two))
    for b in range(8):
        for part in range(2):
            plane = grid[part * NG : part * NG + NG, b * NG : b * NG + NG].reshape(16, NPY, NG)
            for j in range(NCOLD):
                value = jnp.sum(jnp.where(found[j], plane, 0.0), axis=0)
                picked[pl.ds(part * 32 + j * 8 + b, NPY, stride=NG), :] = value
    for s in range(NPY):
        turned = picked[s * NG : s * NG + NG, :].T
        block = turned[0:32] + turned[32:64] + turned[64:96] + turned[96:128]
        back_send[s * NPX : s * NPX + NPX, 0, :] = block + proj_row

    def send_back(to_z, to_y, to_core, to_q):
        to_p = to_z * 4 + (to_y * 2 + to_core)
        row = to_z * 4 + (to_q * NPX + to_y * 2 + to_core)
        remote(back_send.at[row], back_recv.at[owner], back_sems, (to_p, to_q)).start()

    each_other(p, q, send_back)
    own_back = pltpu.make_async_copy(back_send.at[slot], back_recv.at[owner], own_sems.at[3])
    own_back.start()

    own_ca.wait()
    wait_bytes(ca_recv.at[pl.ds(0, NPY - 1)], ca_sems.at[1])
    total = ca_recv[0]
    for s in range(1, NPY):
        total = total + ca_recv[s]
    total = total.reshape(64, NB)
    total = jnp.concatenate([total, jnp.zeros((64, NB), F32)])
    cb_send[...] = total.T.reshape(NPX, 8, NG)

    def send_corr_b(k, carry):
        to_p = partner_px(k, p)
        remote(cb_send.at[to_p], cb_recv.at[p], cb_sems, (to_p, q)).start()
        return carry

    lax.fori_loop(0, NPX - 1, send_corr_b, 0)
    own_cb = pltpu.make_async_copy(cb_send.at[p], cb_recv.at[p], own_sems.at[4])
    own_cb.start()

    own_back.wait()
    wait_bytes(back_recv.at[pl.ds(0, NDEV - 1)], back_sems.at[1])
    low_rows = back_recv[0:NG, 0, :]
    high_rows = back_recv[NG : 2 * NG, 0, :]
    lines = jnp.where(lane < 64, low_rows, pltpu.roll(high_rows, 64, 1)).T
    lines = product(split(lines), pair(mats.at[pl.ds(2, 2)], slice(0, NG)))
    local_re = []
    local_im = []
    for h in range(2):
        res = [lines[h * 64 + j * 8 : h * 64 + j * 8 + 8] for j in range(4)]
        ims = [lines[h * 64 + 32 + j * 8 : h * 64 + 40 + j * 8] for j in range(4)]
        local_re.append(
            jnp.concatenate([r[:, :NG] + i[:, NG:] for r, i in zip(res, ims)], axis=1)
        )
        local_im.append(
            jnp.concatenate([i[:, :NG] - r[:, NG:] for r, i in zip(res, ims)], axis=1)
        )

    proj = jnp.concatenate([low_rows, high_rows])
    proj = pltpu.roll(proj, 64, 1).T[0:32]
    proj_re = proj[0:16]
    proj_im = proj[16:32]
    proj = jnp.concatenate(
        [
            jnp.concatenate([proj_re, -proj_im], axis=1),
            jnp.concatenate([proj_im, proj_re], axis=1),
        ]
    )
    nonlocal_part = product(split(proj), pair(mixed_s))
    psi_re = waves[0, 0:BW, :] * sphere
    psi_im = waves[1, 0:BW, :] * sphere
    hpsi_re = kinetic * psi_re + sphere * jnp.concatenate(local_re) + nonlocal_part[0:16]
    hpsi_im = kinetic * psi_im + sphere * jnp.concatenate(local_im) + nonlocal_part[16:32]
    hpsi_ref[0] = hpsi_re
    hpsi_ref[1] = hpsi_im

    rows = []
    for h in range(2):
        re = hpsi_re[h * 8 : h * 8 + 8]
        im = hpsi_im[h * 8 : h * 8 + 8]
        rows.append(jnp.concatenate([re, im], axis=1))
        rows.append(jnp.concatenate([im, -re], axis=1))
    rows = split(jnp.concatenate(rows))
    rows = tuple(jnp.concatenate([x[0:16]] * 8 + [x[16:32]] * 8) for x in rows)
    partial = product(pair(phi_s), rows, True)
    for h in range(2):
        ham[...] = partial[:, h * NG : h * NG + NG]
        block = jnp.zeros((NPX, NG), F32)
        for m in range(8):
            strip = ham[pl.ds(m, NPX, stride=8), :]
            block = jnp.where(lax.div(lane, 16) == m, strip, block)
        en_send[h * NPX : h * NPX + NPX, 0, :] = block

    def send_energy(to_z, to_y, to_core, to_q):
        to_p = to_z * 4 + (to_y * 2 + to_core)
        row = to_z * 4 + (lax.div(to_q, 4) * NPX + to_y * 2 + to_core)
        remote(en_send.at[row], en_recv.at[slot], en_sems, (to_p, to_q)).start()

    each_other(p, q, send_energy)
    own_en = pltpu.make_async_copy(
        en_send.at[lax.div(q, 4) * NPX + p], en_recv.at[slot], own_sems.at[5]
    )
    own_en.start()

    scale = 1.0 / (NDEV * LOCAL)
    own_cb.wait()
    wait_bytes(cb_recv.at[pl.ds(0, NPX - 1)], cb_sems.at[1])
    total = jnp.sum(cb_recv[...], axis=0) * scale
    corr_ref[0] = total[:, 0:32]
    corr_ref[1] = total[:, 32:64]

    own_en.wait()
    wait_bytes(en_recv.at[pl.ds(0, NDEV - 1)], en_sems.at[1])
    total = jnp.zeros((NPX, NG), F32)
    for s in range(NPY):
        total = total + en_recv[s * NPX : s * NPX + NPX, 0, :]
    total = jnp.sum(total, axis=0, keepdims=True) * scale
    m_row = lax.broadcasted_iota(jnp.int32, (8, NG), 0)
    m_lane = lax.broadcasted_iota(jnp.int32, (8, NG), 1)
    mine = jnp.where(lax.div(m_lane, 16) == m_row, total, 0.0)
    for part in range(2):
        n_first = part * 8 + lax.rem(q, 4) * 2
        for n in range(2):
            one = jnp.where(lax.rem(m_lane, 16) == n_first + n, mine, 0.0)
            energy_ref[part, n : n + 1, :] = jnp.sum(one, axis=1)[None]

    wait_bytes(fwd_send.at[pl.ds(0, NDEV - 1)], fwd_sems.at[0])
    wait_bytes(pot_recv.at[pl.ds(0, NPX - 1)], pot_sems.at[0])
    wait_bytes(ca_send.at[pl.ds(0, NPY - 1)], ca_sems.at[0])
    wait_bytes(cb_send.at[pl.ds(0, NPX - 1)], cb_sems.at[0])
    wait_bytes(back_send.at[pl.ds(0, NDEV - 1)], back_sems.at[0])
    wait_bytes(en_recv.at[pl.ds(0, NDEV - 1)], en_sems.at[0])


def finish(hpsi, corr, energy, hpsi_out, corr_out, energy_out, sems):
    pairs = ((hpsi, hpsi_out), (corr, corr_out), (energy, energy_out))
    copies = [pltpu.make_async_copy(a, b, sems.at[i]) for i, (a, b) in enumerate(pairs)]
    for copy in copies:
        copy.start()
    for copy in copies:
        copy.wait()


def body(waves, col_map, potential, projectors, coupling):
    vmem = pltpu.VMEM
    inside = pl.BlockSpec(memory_space=pltpu.VMEM)
    outside = pl.BlockSpec(memory_space=pltpu.HBM)
    mats = jnp.asarray(dft_tables())
    shapes = (
        jax.ShapeDtypeStruct((2, BW, LOCAL), F32),
        jax.ShapeDtypeStruct((2, 8, 32), F32),
        jax.ShapeDtypeStruct((2, 2, 8), F32),
    )
    arrays = (
        waves,
        col_map,
        jnp.transpose(potential, (1, 2, 0)),
        projectors,
        jnp.transpose(coupling, (1, 2, 0)),
        mats,
    )
    results = pl.pallas_call(
        kernel,
        out_shape=tuple(vmem(x.shape, x.dtype) for x in shapes),
        in_specs=[outside] * 6,
        out_specs=(inside, inside, inside),
        scratch_shapes=[
            vmem((2, NB, LOCAL), F32),
            vmem((2, NB, LOCAL), F32),
            vmem((4, 16, NG), F32),
            vmem((8, 8, 32), F32),
            vmem((2, NG, NG), F32),
            vmem((4, 256, 256), BF16),
            pltpu.SMEM((NCOLD,), jnp.int32),
            vmem((2, NB, 2 * LOCAL), BF16),
            vmem((2, 2 * NB, LOCAL), BF16),
            vmem((2, 2 * NB, LOCAL), BF16),
            vmem((NDEV, 1, NG), F32),
            vmem((NDEV, 1, NG), F32),
            vmem((16, 4, NG), F32),
            vmem((NPX, 4, NG), F32),
            vmem((NPY, 2, 32, NB), F32),
            vmem((NPY, 2, 32, NB), F32),
            vmem((NPX, 8, NG), F32),
            vmem((NPX, 8, NG), F32),
            vmem((NDEV, 1, NG), F32),
            vmem((NDEV, 1, NG), F32),
            vmem((2 * NPX, 1, NG), F32),
            vmem((NDEV, 1, NG), F32),
            vmem((NPY * NG, NG), F32),
            vmem((2 * NG, 8 * NG), F32),
            vmem((2 * NG, 8 * NG), F32),
            vmem((NPY * NG, NG), F32),
            vmem((NB, NG), F32),
            vmem((2, 8 * NG, 256), BF16),
            vmem((2, 8 * NG, 256), BF16),
            pltpu.SemaphoreType.DMA((7,)),
            pltpu.SemaphoreType.DMA((6,)),
            pltpu.SemaphoreType.DMA((2,)),
            pltpu.SemaphoreType.DMA((2,)),
            pltpu.SemaphoreType.DMA((2,)),
            pltpu.SemaphoreType.DMA((2,)),
            pltpu.SemaphoreType.DMA((2,)),
            pltpu.SemaphoreType.DMA((2,)),
        ],
        compiler_params=pltpu.CompilerParams(
            collective_id=0, has_side_effects=True, vmem_limit_bytes=40 << 20
        ),
        name="hamiltonian",
    )(*(pltpu.with_memory_space_constraint(x, pltpu.HBM) for x in arrays))
    hpsi, corr, energy = pl.pallas_call(
        finish,
        out_shape=shapes,
        in_specs=[inside] * 3,
        out_specs=(outside, outside, outside),
        scratch_shapes=[pltpu.SemaphoreType.DMA((3,))],
        name="finish",
    )(*(pltpu.with_memory_space_constraint(x, pltpu.VMEM) for x in results))
    return hpsi, corr, jnp.transpose(energy, (0, 2, 1))


def solution(mesh):
    placed = (
        P(None, None, ("px", "py")),
        P(("px", "py")),
        P(None, "px", "py"),
        P(None, None, ("px", "py")),
        P(),
    )
    return jax.shard_map(
        body,
        mesh=mesh,
        in_specs=placed,
        out_specs=(P(None, None, ("px", "py")), P(None, "px", "py"), P(None, "px", "py")),
        check_vma=False,
    )
```

```python
import math

import jax
import jax.numpy as jnp
import numpy as np
from jax import lax
from jax.experimental import pallas as pl
from jax.experimental.pallas import tpu as pltpu
from jax.sharding import PartitionSpec as P

NG = 128
NB = 256
BW = 16
NCOLD = 4
GCUT = 50
NPX = 32
NPY = 8
NDEV = NPX * NPY
LOCAL = NCOLD * NG
MESH = pl.DeviceIdType.MESH
F32 = jnp.float32
BF16 = jnp.bfloat16


def dft_tables():
    index = np.arange(NG)
    angle = (index[:, None] * index[None, :] % NG) * (2.0 * math.pi / NG)
    return np.stack([np.cos(angle), np.sin(angle)]).astype(np.float32) / np.float32(math.sqrt(NG))


def split(x):
    high = x.astype(BF16)
    return high, (x - high.astype(F32)).astype(BF16)


def product(a, b, transposed=False):
    left = jnp.concatenate([a[0], a[0], a[1]], axis=1)
    right = jnp.concatenate([b[0], b[1], b[0]], axis=1 if transposed else 0)
    dims = (((1,), (1 if transposed else 0,)), ((), ()))
    return lax.dot_general(left, right, dims, preferred_element_type=F32)


def pair(ref, *index):
    return ref[(0, *index)], ref[(1, *index)]


def store(ref, row, parts):
    for i, part in enumerate(parts):
        ref[i, row : row + part.shape[0], :] = part


def far_first(digit, half):
    odd = lax.rem(digit, 2)
    return half + (1 - 2 * odd) * lax.div(digit + 1, 2)


def partner_px(k, p):
    z = lax.rem(lax.div(p, 4) + far_first(lax.div(k, 4), 4), 8)
    y_lo = lax.rem(lax.div(p, 2) + 1 + lax.rem(lax.div(k, 2), 2), 2)
    core = lax.rem(p + 1 + lax.rem(k, 2), 2)
    return z * 4 + y_lo * 2 + core


def partner_py(k, q):
    x = lax.rem(lax.div(q, 2) + far_first(lax.div(k, 2), 2), 4)
    y_hi = lax.rem(q + 1 + lax.rem(k, 2), 2)
    return x * 2 + y_hi


def each_other(p, q, visit):
    z = lax.div(p, 4)
    y_lo = lax.rem(lax.div(p, 2), 2)
    core = lax.rem(p, 2)
    x = lax.div(q, 2)
    y_hi = lax.rem(q, 2)
    to_z = [lax.rem(z + d, 8) for d in range(8)]
    to_y = [y_lo, 1 - y_lo]
    to_core = [core, 1 - core]
    to_q = [[lax.rem(x + d, 4) * 2 + h for h in (y_hi, 1 - y_hi)] for d in range(4)]
    hops = []
    for dz, dx, hi, lo, dc in np.ndindex(8, 4, 2, 2, 2):
        far = min(dz, 8 - dz) + min(dx, 4 - dx) + (1 if lo else 2 * hi) + 0.6 * dc
        hops.append((-far, dz, dx, hi, lo, dc))
    for _, dz, dx, hi, lo, dc in sorted(hops)[:-1]:
        visit(to_z[dz], to_y[lo], to_core[dc], to_q[dx][hi])


def remote(src, dst, sems, place):
    return pltpu.make_async_remote_copy(
        src_ref=src,
        dst_ref=dst,
        send_sem=sems.at[0],
        recv_sem=sems.at[1],
        device_id=place,
        device_id_type=MESH,
    )


def wait_bytes(ref, sem):
    pltpu.make_async_copy(ref, ref, sem).wait()


def kernel(
    waves_hbm,
    col_hbm,
    pot_hbm,
    beta_hbm,
    coup_hbm,
    mats_hbm,
    hpsi_ref,
    corr_ref,
    energy_ref,
    waves,
    beta,
    pot,
    coup,
    tables,
    mats,
    col,
    phi_s,
    beta_s,
    mixed_s,
    fwd_send,
    fwd_recv,
    pot_send,
    pot_recv,
    ca_send,
    ca_recv,
    cb_send,
    cb_recv,
    back_send,
    back_recv,
    en_send,
    en_recv,
    unpack,
    field,
    grid,
    picked,
    ham,
    lines_s,
    real_s,
    load_sems,
    own_sems,
    fwd_sems,
    pot_sems,
    ca_sems,
    cb_sems,
    back_sems,
    en_sems,
):
    p = lax.axis_index("px")
    q = lax.axis_index("py")
    z_low = lax.div(p, 2)
    half = lax.rem(p, 2)
    owner = half * NG + q * 16 + z_low
    slot = q * NPX + p

    barrier = pltpu.get_barrier_semaphore()

    def greet(to_z, to_y, to_core, to_q):
        to_p = to_z * 4 + (to_y * 2 + to_core)
        pl.semaphore_signal(barrier, inc=1, device_id=(to_p, to_q), device_id_type=MESH)

    loads = [
        (waves_hbm.at[:, pl.ds(0, BW)], waves.at[:, pl.ds(0, BW)]),
        (mats_hbm, tables),
        (col_hbm, col),
        (beta_hbm, beta),
        (waves_hbm.at[:, pl.ds(BW, NB - BW)], waves.at[:, pl.ds(BW, NB - BW)]),
        (pot_hbm, pot),
        (coup_hbm, coup),
    ]
    loads = [pltpu.make_async_copy(s, d, load_sems.at[i]) for i, (s, d) in enumerate(loads)]
    for load in loads:
        load.start()
    each_other(p, q, greet)

    lane = lax.broadcasted_iota(jnp.int32, (1, NG), 1)

    loads[0].wait()
    loads[1].wait()
    loads[2].wait()
    z_freq = jnp.where(lane < NG // 2, lane, lane - NG)
    spheres = []
    kinetics = []
    cols = jnp.zeros((1, NG), F32)
    for j in range(NCOLD):
        place = col[j]
        cols = jnp.where(lane == 96 + j, place.astype(F32), cols)
        x = p + NPX * lax.div(place, 16)
        y = q + NPY * lax.rem(place, 16)
        fx = jnp.where(x < NG // 2, x, x - NG)
        fy = jnp.where(y < NG // 2, y, y - NG)
        square = fx * fx + fy * fy + z_freq * z_freq
        spheres.append(jnp.where(square <= GCUT * GCUT, 1.0, 0.0).astype(F32))
        kinetics.append(square.astype(F32) * (2.0 / (NG * NG)))
    sphere = jnp.concatenate(spheres, axis=1)
    kinetic = jnp.concatenate(kinetics, axis=1)

    cosine = tables[0]
    sine = tables[1]
    for i, lower in enumerate((sine, -sine)):
        table = jnp.concatenate(
            [
                jnp.concatenate([cosine, -lower], axis=1),
                jnp.concatenate([lower, cosine], axis=1),
            ]
        )
        high, low = split(table)
        mats[2 * i] = high
        mats[2 * i + 1] = low

    psi_re = waves[0, 0:BW, :] * sphere
    psi_im = waves[1, 0:BW, :] * sphere
    rows = []
    for h in range(2):
        for part in range(2):
            for j in range(NCOLD):
                re = psi_re[h * 8 : h * 8 + 8, j * NG : j * NG + NG]
                im = psi_im[h * 8 : h * 8 + 8, j * NG : j * NG + NG]
                rows.append(jnp.concatenate([re, -im] if part == 0 else [im, re], axis=1))
    z_rows = product(pair(mats.at[pl.ds(2, 2)], slice(0, NG)), split(jnp.concatenate(rows)), True)

    loads[3].wait()
    for part in range(2):
        high, low = split(beta[part] * sphere)
        beta_s[0, part * NB : part * NB + NB, :] = high
        beta_s[1, part * NB : part * NB + NB, :] = low
    zeros = jnp.zeros((32, LOCAL), F32)
    with_re = split(jnp.concatenate([zeros, zeros, psi_re, psi_im, zeros]))
    with_im = split(jnp.concatenate([zeros, zeros, psi_im, -psi_re, zeros]))
    partial = product(pair(beta_s, slice(0, NB)), with_re, True) + product(
        pair(beta_s, slice(NB, 2 * NB)), with_im, True
    )
    for h in range(2):
        part = pltpu.roll(z_rows, 64, 1) if h else z_rows
        rows = jnp.where(lane < 64, part, partial[h * NG : h * NG + NG]) + cols
        fwd_send[h * NG : h * NG + NG, :] = rows

    loads[5].wait()
    for y in range(4):
        pot_send[:, y, :] = pot[y]

    pl.semaphore_wait(barrier, NDEV - 1)

    def send_forward(to_z, to_y, to_core, to_q):
        to_p = to_z * 4 + (to_y * 2 + to_core)
        row = to_z * 2 + (to_core * NG + to_q * 16 + to_y)
        remote(fwd_send.at[pl.ds(row, 1)], fwd_recv.at[pl.ds(slot, 1)], fwd_sems, (to_p, to_q)).start()

    each_other(p, q, send_forward)
    own_forward = pltpu.make_async_copy(fwd_send.at[pl.ds(owner, 1)], fwd_recv.at[pl.ds(slot, 1)], own_sems.at[0])
    own_forward.start()

    def send_potential(k, carry):
        to_p = partner_px(k, p)
        remote(pot_send.at[lax.div(to_p, 2)], pot_recv.at[p], pot_sems, (to_p, q)).start()
        return carry

    lax.fori_loop(0, NPX - 1, send_potential, 0)
    own_pot = pltpu.make_async_copy(pot_send.at[z_low], pot_recv.at[p], own_sems.at[1])
    own_pot.start()

    loads[4].wait()
    for part in range(2):
        high, low = split(waves[part] * sphere)
        phi_s[0, :, part * LOCAL : part * LOCAL + LOCAL] = high
        phi_s[1, :, part * LOCAL : part * LOCAL + LOCAL] = low
    phi = pair(phi_s)
    turned = tuple(jnp.concatenate([-x[:, LOCAL:], x[:, :LOCAL]], axis=1) for x in phi)
    ca_send[:, 0] = product(phi, phi, True).reshape(NPY, 32, NB)
    ca_send[:, 1] = product(phi, turned, True).reshape(NPY, 32, NB)

    def send_corr_a(k, carry):
        to_q = partner_py(k, q)
        remote(ca_send.at[to_q], ca_recv.at[q], ca_sems, (p, to_q)).start()
        return carry

    lax.fori_loop(0, NPY - 1, send_corr_a, 0)
    own_ca = pltpu.make_async_copy(ca_send.at[q], ca_recv.at[q], own_sems.at[2])
    own_ca.start()

    loads[6].wait()
    pick_row = lax.broadcasted_iota(jnp.int32, (32, NB), 0)
    pick_lane = lax.broadcasted_iota(jnp.int32, (32, NB), 1)
    pick = jnp.where(lax.div(pick_lane, 8) == pick_row, 1.0, 0.0).astype(F32)
    wide = jnp.dot(
        coup[...].reshape(64, 32), pick, precision=lax.Precision.HIGHEST, preferred_element_type=F32
    )
    blk_j = lax.broadcasted_iota(jnp.int32, (8, 8, NB), 1)
    blk_lane = lax.broadcasted_iota(jnp.int32, (8, 8, NB), 2)
    wide = jnp.where(lax.rem(blk_lane, 8) == blk_j, wide.reshape(8, 8, NB), 0.0)
    wide = jnp.concatenate([jnp.sum(wide, axis=1)] * 32)
    sym_row = lax.broadcasted_iota(jnp.int32, (NB, NB), 0)
    sym_lane = lax.broadcasted_iota(jnp.int32, (NB, NB), 1)
    wide = jnp.where(lax.div(sym_row, 8) == lax.div(sym_lane, 8), wide, 0.0)
    high, low = split(0.5 * (wide + wide.T))
    for part in range(2):
        rows = slice(part * NB, part * NB + NB)
        store(mixed_s, part * NB, split(product((high, low), pair(beta_s, rows))))
    picked[...] = jnp.zeros((NPY * NG, NG), F32)

    own_forward.wait()
    wait_bytes(fwd_recv.at[pl.ds(0, NDEV - 1)], fwd_sems.at[1])
    proj_sum = jnp.zeros((NPX, NG), F32)
    for s in range(NPY):
        block = fwd_recv[s * NPX : s * NPX + NPX, :]
        proj_sum = proj_sum + block
        unpack[s * NG : s * NG + NG, :] = jnp.concatenate([block] * 4).T
    proj_sum = jnp.sum(proj_sum, axis=0, keepdims=True)
    proj_row = jnp.where((lane >= 64) & (lane < 96), proj_sum, 0.0)
    x_slot = lax.div(lane, 32).astype(F32) * 16.0
    y_slot = lax.broadcasted_iota(jnp.int32, (16, NPY, NG), 0).astype(F32)
    found = []
    for j in range(NCOLD):
        place = unpack[pl.ds(96 + j, NPY, stride=NG), :] - x_slot
        found.append(y_slot == place[None])
    for b in range(8):
        for part in range(2):
            plane = jnp.zeros((16, NPY, NG), F32)
            for j in range(NCOLD):
                value = unpack[pl.ds(part * 32 + j * 8 + b, NPY, stride=NG), :]
                plane = jnp.where(found[j], value[None], plane)
            field[part * NG : part * NG + NG, b * NG : b * NG + NG] = plane.reshape(NG, NG)

    own_pot.wait()
    wait_bytes(pot_recv.at[pl.ds(0, NPX - 1)], pot_sems.at[1])
    potential = pot_recv[...].reshape(NG, NG)
    potential = jnp.concatenate([potential, potential], axis=1)
    potential = jnp.concatenate([potential, potential])
    mat_a = pair(mats.at[pl.ds(0, 2)])
    mat_b = pair(mats.at[pl.ds(2, 2)])
    for c in range(4):
        two = slice(c * 256, c * 256 + 256)
        lines = product(mat_a, split(field[:, two]))
        for b in range(2):
            part = lines[:, b * NG : b * NG + NG]
            row = (2 * c + b) * NG
            store(lines_s, row, split(jnp.concatenate([part[:NG], part[NG:]], axis=1)))
    for c in range(4):
        two = slice(c * 256, c * 256 + 256)
        real = product(pair(lines_s, two), mat_b) * potential
        store(real_s, c * 256, split(real))
    for c in range(4):
        two = slice(c * 256, c * 256 + 256)
        back = product(pair(real_s, two), mat_a)
        columns = []
        for b in range(2):
            part = back[b * NG : b * NG + NG]
            columns.append(jnp.concatenate([part[:, :NG], part[:, NG:]]))
        store(lines_s, c * 256, split(jnp.concatenate(columns, axis=1)))
    for c in range(4):
        two = slice(c * 256, c * 256 + 256)
        grid[:, two] = product(mat_b, pair(lines_s, two))
    for b in range(8):
        for part in range(2):
            plane = grid[part * NG : part * NG + NG, b * NG : b * NG + NG].reshape(16, NPY, NG)
            for j in range(NCOLD):
                value = jnp.sum(jnp.where(found[j], plane, 0.0), axis=0)
                picked[pl.ds(part * 32 + j * 8 + b, NPY, stride=NG), :] = value
    for s in range(NPY):
        turned = picked[s * NG : s * NG + NG, :].T
        block = turned[0:32] + turned[32:64] + turned[64:96] + turned[96:128]
        back_send[s * NPX : s * NPX + NPX, :] = block + proj_row

    def send_back(to_z, to_y, to_core, to_q):
        to_p = to_z * 4 + (to_y * 2 + to_core)
        row = to_z * 4 + (to_q * NPX + to_y * 2 + to_core)
        remote(back_send.at[pl.ds(row, 1)], back_recv.at[pl.ds(owner, 1)], back_sems, (to_p, to_q)).start()

    each_other(p, q, send_back)
    own_back = pltpu.make_async_copy(back_send.at[pl.ds(slot, 1)], back_recv.at[pl.ds(owner, 1)], own_sems.at[3])
    own_back.start()

    own_ca.wait()
    wait_bytes(ca_recv.at[pl.ds(0, NPY - 1)], ca_sems.at[1])
    total = ca_recv[0]
    for s in range(1, NPY):
        total = total + ca_recv[s]
    total = total.reshape(64, NB)
    total = jnp.concatenate([total, jnp.zeros((64, NB), F32)])
    cb_send[...] = total.T.reshape(NPX, 8, NG)

    def send_corr_b(k, carry):
        to_p = partner_px(k, p)
        remote(cb_send.at[to_p], cb_recv.at[p], cb_sems, (to_p, q)).start()
        return carry

    lax.fori_loop(0, NPX - 1, send_corr_b, 0)
    own_cb = pltpu.make_async_copy(cb_send.at[p], cb_recv.at[p], own_sems.at[4])
    own_cb.start()

    own_back.wait()
    wait_bytes(back_recv.at[pl.ds(0, NDEV - 1)], back_sems.at[1])
    low_rows = back_recv[0:NG, :]
    high_rows = back_recv[NG : 2 * NG, :]
    lines = jnp.where(lane < 64, low_rows, pltpu.roll(high_rows, 64, 1)).T
    lines = product(split(lines), pair(mats.at[pl.ds(2, 2)], slice(0, NG)))
    local_re = []
    local_im = []
    for h in range(2):
        res = [lines[h * 64 + j * 8 : h * 64 + j * 8 + 8] for j in range(4)]
        ims = [lines[h * 64 + 32 + j * 8 : h * 64 + 40 + j * 8] for j in range(4)]
        local_re.append(
            jnp.concatenate([r[:, :NG] + i[:, NG:] for r, i in zip(res, ims)], axis=1)
        )
        local_im.append(
            jnp.concatenate([i[:, :NG] - r[:, NG:] for r, i in zip(res, ims)], axis=1)
        )

    proj = jnp.concatenate([low_rows, high_rows])
    proj = pltpu.roll(proj, 64, 1).T[0:32]
    proj_re = proj[0:16]
    proj_im = proj[16:32]
    proj = jnp.concatenate(
        [
            jnp.concatenate([proj_re, -proj_im], axis=1),
            jnp.concatenate([proj_im, proj_re], axis=1),
        ]
    )
    high, low = split(proj)
    mixed = pair(mixed_s)
    stacked = jnp.dot(jnp.concatenate([high, low]), mixed[0], preferred_element_type=F32)
    nonlocal_part = jnp.dot(high, mixed[1], preferred_element_type=F32)
    nonlocal_part = stacked[0:32] + stacked[32:64] + nonlocal_part
    psi_re = waves[0, 0:BW, :] * sphere
    psi_im = waves[1, 0:BW, :] * sphere
    hpsi_re = kinetic * psi_re + sphere * jnp.concatenate(local_re) + nonlocal_part[0:16]
    hpsi_im = kinetic * psi_im + sphere * jnp.concatenate(local_im) + nonlocal_part[16:32]
    hpsi_ref[0] = hpsi_re
    hpsi_ref[1] = hpsi_im

    rows = []
    for h in range(2):
        re = hpsi_re[h * 8 : h * 8 + 8]
        im = hpsi_im[h * 8 : h * 8 + 8]
        rows.append(jnp.concatenate([re, im], axis=1))
        rows.append(jnp.concatenate([im, -re], axis=1))
    high, low = split(jnp.concatenate(rows))
    phi = pair(phi_s)
    dims = (((1,), (1,)), ((), ()))
    both = jnp.concatenate([high, low, jnp.zeros((64, 2 * LOCAL), BF16)])
    both = lax.dot_general(phi[0], both, dims, preferred_element_type=F32)
    high = jnp.concatenate([high, jnp.zeros((96, 2 * LOCAL), BF16)])
    rest = lax.dot_general(phi[1], high, dims, preferred_element_type=F32)
    ham[...] = both + pltpu.roll(both, 96, 1) + rest
    for h in range(2):
        block = jnp.zeros((NPX, NG), F32)
        for m in range(8):
            strip = pltpu.roll(ham[pl.ds(m, NPX, stride=8), :], (m - h) * 16 % NG, 1)
            block = jnp.where(lax.div(lane, 16) == m, strip, block)
        en_send[h * NPX : h * NPX + NPX, :] = block

    def send_energy(to_z, to_y, to_core, to_q):
        to_p = to_z * 4 + (to_y * 2 + to_core)
        row = to_z * 4 + (lax.div(to_q, 4) * NPX + to_y * 2 + to_core)
        remote(en_send.at[pl.ds(row, 1)], en_recv.at[pl.ds(slot, 1)], en_sems, (to_p, to_q)).start()

    each_other(p, q, send_energy)
    own_en = pltpu.make_async_copy(
        en_send.at[pl.ds(lax.div(q, 4) * NPX + p, 1)], en_recv.at[pl.ds(slot, 1)], own_sems.at[5]
    )
    own_en.start()

    scale = 1.0 / (NDEV * LOCAL)
    own_cb.wait()
    wait_bytes(cb_recv.at[pl.ds(0, NPX - 1)], cb_sems.at[1])
    total = jnp.sum(cb_recv[...], axis=0) * scale
    corr_ref[0] = total[:, 0:32]
    corr_ref[1] = total[:, 32:64]

    own_en.wait()
    wait_bytes(en_recv.at[pl.ds(0, NDEV - 1)], en_sems.at[1])
    total = jnp.zeros((NPX, NG), F32)
    for s in range(NPY):
        total = total + en_recv[s * NPX : s * NPX + NPX, :]
    total = jnp.sum(total, axis=0, keepdims=True) * scale
    m_row = lax.broadcasted_iota(jnp.int32, (8, NG), 0)
    m_lane = lax.broadcasted_iota(jnp.int32, (8, NG), 1)
    mine = jnp.where(lax.div(m_lane, 16) == m_row, total, 0.0)
    for part in range(2):
        n_first = part * 8 + lax.rem(q, 4) * 2
        for n in range(2):
            one = jnp.where(lax.rem(m_lane, 16) == n_first + n, mine, 0.0)
            energy_ref[part, n : n + 1, :] = jnp.sum(one, axis=1)[None]

    wait_bytes(fwd_send.at[pl.ds(0, NDEV - 1)], fwd_sems.at[0])
    wait_bytes(pot_recv.at[pl.ds(0, NPX - 1)], pot_sems.at[0])
    wait_bytes(ca_send.at[pl.ds(0, NPY - 1)], ca_sems.at[0])
    wait_bytes(cb_send.at[pl.ds(0, NPX - 1)], cb_sems.at[0])
    wait_bytes(back_send.at[pl.ds(0, NDEV - 1)], back_sems.at[0])
    wait_bytes(en_recv.at[pl.ds(0, NDEV - 1)], en_sems.at[0])


def finish(hpsi, corr, energy, hpsi_out, corr_out, energy_out, sems):
    pairs = ((hpsi, hpsi_out), (corr, corr_out), (energy, energy_out))
    copies = [pltpu.make_async_copy(a, b, sems.at[i]) for i, (a, b) in enumerate(pairs)]
    for copy in copies:
        copy.start()
    for copy in copies:
        copy.wait()


def body(waves, col_map, potential, projectors, coupling):
    vmem = pltpu.VMEM
    inside = pl.BlockSpec(memory_space=pltpu.VMEM)
    outside = pl.BlockSpec(memory_space=pltpu.HBM)
    mats = jnp.asarray(dft_tables())
    shapes = (
        jax.ShapeDtypeStruct((2, BW, LOCAL), F32),
        jax.ShapeDtypeStruct((2, 8, 32), F32),
        jax.ShapeDtypeStruct((2, 2, 8), F32),
    )
    arrays = (
        waves,
        col_map,
        jnp.transpose(potential, (1, 2, 0)),
        projectors,
        jnp.transpose(coupling, (1, 2, 0)),
        mats,
    )
    results = pl.pallas_call(
        kernel,
        out_shape=tuple(vmem(x.shape, x.dtype) for x in shapes),
        in_specs=[outside] * 6,
        out_specs=(inside, inside, inside),
        scratch_shapes=[
            vmem((2, NB, LOCAL), F32),
            vmem((2, NB, LOCAL), F32),
            vmem((4, 16, NG), F32),
            vmem((8, 8, 32), F32),
            vmem((2, NG, NG), F32),
            vmem((4, 256, 256), BF16),
            pltpu.SMEM((NCOLD,), jnp.int32),
            vmem((2, NB, 2 * LOCAL), BF16),
            vmem((2, 2 * NB, LOCAL), BF16),
            vmem((2, 2 * NB, LOCAL), BF16),
            vmem((NDEV, NG), F32),
            vmem((NDEV, NG), F32),
            vmem((16, 4, NG), F32),
            vmem((NPX, 4, NG), F32),
            vmem((NPY, 2, 32, NB), F32),
            vmem((NPY, 2, 32, NB), F32),
            vmem((NPX, 8, NG), F32),
            vmem((NPX, 8, NG), F32),
            vmem((NDEV, NG), F32),
            vmem((NDEV, NG), F32),
            vmem((2 * NPX, NG), F32),
            vmem((NDEV, NG), F32),
            vmem((NPY * NG, NG), F32),
            vmem((2 * NG, 8 * NG), F32),
            vmem((2 * NG, 8 * NG), F32),
            vmem((NPY * NG, NG), F32),
            vmem((NB, NG), F32),
            vmem((2, 8 * NG, 256), BF16),
            vmem((2, 8 * NG, 256), BF16),
            pltpu.SemaphoreType.DMA((7,)),
            pltpu.SemaphoreType.DMA((6,)),
            pltpu.SemaphoreType.DMA((2,)),
            pltpu.SemaphoreType.DMA((2,)),
            pltpu.SemaphoreType.DMA((2,)),
            pltpu.SemaphoreType.DMA((2,)),
            pltpu.SemaphoreType.DMA((2,)),
            pltpu.SemaphoreType.DMA((2,)),
        ],
        compiler_params=pltpu.CompilerParams(
            collective_id=0, has_side_effects=True, vmem_limit_bytes=40 << 20
        ),
        name="hamiltonian",
    )(*(pltpu.with_memory_space_constraint(x, pltpu.HBM) for x in arrays))
    hpsi, corr, energy = pl.pallas_call(
        finish,
        out_shape=shapes,
        in_specs=[inside] * 3,
        out_specs=(outside, outside, outside),
        scratch_shapes=[pltpu.SemaphoreType.DMA((3,))],
        name="finish",
    )(*(pltpu.with_memory_space_constraint(x, pltpu.VMEM) for x in results))
    return hpsi, corr, jnp.transpose(energy, (0, 2, 1))


def solution(mesh):
    placed = (
        P(None, None, ("px", "py")),
        P(("px", "py")),
        P(None, "px", "py"),
        P(None, None, ("px", "py")),
        P(),
    )
    return jax.shard_map(
        body,
        mesh=mesh,
        in_specs=placed,
        out_specs=(P(None, None, ("px", "py")), P(None, "px", "py"), P(None, "px", "py")),
        check_vma=False,
    )
```

```python
import math

import jax
import jax.numpy as jnp
import numpy as np
from jax import lax
from jax.experimental import pallas as pl
from jax.experimental.pallas import tpu as pltpu
from jax.sharding import PartitionSpec as P

NG = 128
NB = 256
BW = 16
NCOLD = 4
GCUT = 50
NPX = 32
NPY = 8
NDEV = NPX * NPY
LOCAL = NCOLD * NG
MESH = pl.DeviceIdType.MESH
F32 = jnp.float32
BF16 = jnp.bfloat16


def dft_tables():
    index = np.arange(NG)
    angle = (index[:, None] * index[None, :] % NG) * (2.0 * math.pi / NG)
    return np.stack([np.cos(angle), np.sin(angle)]).astype(np.float32) / np.float32(math.sqrt(NG))


def split(x):
    high = x.astype(BF16)
    return high, (x - high.astype(F32)).astype(BF16)


def product(a, b, transposed=False):
    left = jnp.concatenate([a[0], a[0], a[1]], axis=1)
    right = jnp.concatenate([b[0], b[1], b[0]], axis=1 if transposed else 0)
    dims = (((1,), (1 if transposed else 0,)), ((), ()))
    return lax.dot_general(left, right, dims, preferred_element_type=F32)


def pair(ref, *index):
    return ref[(0, *index)], ref[(1, *index)]


def store(ref, row, parts):
    for i, part in enumerate(parts):
        ref[i, row : row + part.shape[0], :] = part


def far_first(digit, half):
    odd = lax.rem(digit, 2)
    return half + (1 - 2 * odd) * lax.div(digit + 1, 2)


def partner_py(k, q):
    x = lax.rem(lax.div(q, 2) + far_first(lax.div(k, 2), 2), 4)
    y_hi = lax.rem(q + 1 + lax.rem(k, 2), 2)
    return x * 2 + y_hi


def along_px(p):
    z = lax.div(p, 4)
    y_lo = lax.rem(lax.div(p, 2), 2)
    core = lax.rem(p, 2)
    to_z = [lax.rem(z + d, 8) for d in range(8)]
    to_y = [y_lo, 1 - y_lo]
    to_core = [core, 1 - core]
    hops = []
    for dz, lo, dc in np.ndindex(8, 2, 2):
        hops.append((-(min(dz, 8 - dz) + lo + 0.6 * dc), dz, lo, dc))
    return [(to_z[dz], to_y[lo], to_core[dc]) for _, dz, lo, dc in sorted(hops)[:-1]]


def each_other(p, q, visit):
    z = lax.div(p, 4)
    y_lo = lax.rem(lax.div(p, 2), 2)
    core = lax.rem(p, 2)
    x = lax.div(q, 2)
    y_hi = lax.rem(q, 2)
    to_z = [lax.rem(z + d, 8) for d in range(8)]
    to_y = [y_lo, 1 - y_lo]
    to_core = [core, 1 - core]
    to_q = [[lax.rem(x + d, 4) * 2 + h for h in (y_hi, 1 - y_hi)] for d in range(4)]
    hops = []
    for dz, dx, hi, lo, dc in np.ndindex(8, 4, 2, 2, 2):
        far = min(dz, 8 - dz) + min(dx, 4 - dx) + (1 if lo else 2 * hi) + 0.6 * dc
        hops.append((-far, dz, dx, hi, lo, dc))
    for _, dz, dx, hi, lo, dc in sorted(hops)[:-1]:
        visit(to_z[dz], to_y[lo], to_core[dc], to_q[dx][hi])


def remote(src, dst, sems, place):
    return pltpu.make_async_remote_copy(
        src_ref=src,
        dst_ref=dst,
        send_sem=sems.at[0],
        recv_sem=sems.at[1],
        device_id=place,
        device_id_type=MESH,
    )


def wait_bytes(ref, sem):
    pltpu.make_async_copy(ref, ref, sem).wait()


def kernel(
    waves_hbm,
    col_hbm,
    pot_hbm,
    beta_hbm,
    coup_hbm,
    mats_hbm,
    hpsi_ref,
    corr_ref,
    energy_ref,
    waves,
    beta,
    pot,
    coup,
    tables,
    mats,
    col,
    phi_s,
    beta_s,
    mixed_s,
    fwd_send,
    fwd_recv,
    pot_send,
    pot_recv,
    ca_send,
    ca_recv,
    cb_send,
    cb_recv,
    back_send,
    back_recv,
    en_send,
    en_recv,
    unpack,
    field,
    grid,
    picked,
    ham,
    lines_s,
    real_s,
    load_sems,
    own_sems,
    fwd_sems,
    pot_sems,
    ca_sems,
    cb_sems,
    back_sems,
    en_sems,
):
    p = lax.axis_index("px")
    q = lax.axis_index("py")
    z_low = lax.div(p, 2)
    half = lax.rem(p, 2)
    owner = half * NG + q * 16 + z_low
    slot = q * NPX + p

    barrier = pltpu.get_barrier_semaphore()

    def greet(to_z, to_y, to_core, to_q):
        to_p = to_z * 4 + (to_y * 2 + to_core)
        pl.semaphore_signal(barrier, inc=1, device_id=(to_p, to_q), device_id_type=MESH)

    loads = [
        (waves_hbm.at[:, pl.ds(0, BW)], waves.at[:, pl.ds(0, BW)]),
        (mats_hbm, tables),
        (col_hbm, col),
        (beta_hbm, beta),
        (waves_hbm.at[:, pl.ds(BW, NB - BW)], waves.at[:, pl.ds(BW, NB - BW)]),
        (pot_hbm, pot),
        (coup_hbm, coup),
    ]
    loads = [pltpu.make_async_copy(s, d, load_sems.at[i]) for i, (s, d) in enumerate(loads)]
    for load in loads:
        load.start()
    each_other(p, q, greet)

    lane = lax.broadcasted_iota(jnp.int32, (1, NG), 1)

    loads[0].wait()
    loads[1].wait()
    loads[2].wait()
    z_freq = jnp.where(lane < NG // 2, lane, lane - NG)
    spheres = []
    kinetics = []
    cols = jnp.zeros((1, NG), F32)
    for j in range(NCOLD):
        place = col[j]
        cols = jnp.where(lane == 96 + j, place.astype(F32), cols)
        x = p + NPX * lax.div(place, 16)
        y = q + NPY * lax.rem(place, 16)
        fx = jnp.where(x < NG // 2, x, x - NG)
        fy = jnp.where(y < NG // 2, y, y - NG)
        square = fx * fx + fy * fy + z_freq * z_freq
        spheres.append(jnp.where(square <= GCUT * GCUT, 1.0, 0.0).astype(F32))
        kinetics.append(square.astype(F32) * (2.0 / (NG * NG)))
    sphere = jnp.concatenate(spheres, axis=1)
    kinetic = jnp.concatenate(kinetics, axis=1)

    cosine = tables[0]
    sine = tables[1]
    for i, lower in enumerate((sine, -sine)):
        table = jnp.concatenate(
            [
                jnp.concatenate([cosine, -lower], axis=1),
                jnp.concatenate([lower, cosine], axis=1),
            ]
        )
        high, low = split(table)
        mats[2 * i] = high
        mats[2 * i + 1] = low

    psi_re = waves[0, 0:BW, :] * sphere
    psi_im = waves[1, 0:BW, :] * sphere
    rows = []
    for h in range(2):
        for part in range(2):
            for j in range(NCOLD):
                re = psi_re[h * 8 : h * 8 + 8, j * NG : j * NG + NG]
                im = psi_im[h * 8 : h * 8 + 8, j * NG : j * NG + NG]
                rows.append(jnp.concatenate([re, -im] if part == 0 else [im, re], axis=1))
    z_rows = product(pair(mats.at[pl.ds(2, 2)], slice(0, NG)), split(jnp.concatenate(rows)), True)

    loads[3].wait()
    for part in range(2):
        high, low = split(beta[part] * sphere)
        beta_s[0, part * NB : part * NB + NB, :] = high
        beta_s[1, part * NB : part * NB + NB, :] = low
    zeros = jnp.zeros((32, LOCAL), F32)
    with_re = split(jnp.concatenate([zeros, zeros, psi_re, psi_im, zeros]))
    with_im = split(jnp.concatenate([zeros, zeros, psi_im, -psi_re, zeros]))
    partial = product(pair(beta_s, slice(0, NB)), with_re, True) + product(
        pair(beta_s, slice(NB, 2 * NB)), with_im, True
    )
    for h in range(2):
        part = pltpu.roll(z_rows, 64, 1) if h else z_rows
        rows = jnp.where(lane < 64, part, partial[h * NG : h * NG + NG]) + cols
        fwd_send[h * NG : h * NG + NG, :] = rows

    loads[5].wait()
    for y in range(4):
        pot_send[:, y, :] = pot[y]

    pl.semaphore_wait(barrier, NDEV - 1)

    def send_forward(to_z, to_y, to_core, to_q):
        to_p = to_z * 4 + (to_y * 2 + to_core)
        row = to_z * 2 + (to_core * NG + to_q * 16 + to_y)
        remote(fwd_send.at[pl.ds(row, 1)], fwd_recv.at[pl.ds(slot, 1)], fwd_sems, (to_p, to_q)).start()

    each_other(p, q, send_forward)
    own_forward = pltpu.make_async_copy(fwd_send.at[pl.ds(owner, 1)], fwd_recv.at[pl.ds(slot, 1)], own_sems.at[0])
    own_forward.start()

    for to_z, to_y, to_core in along_px(p):
        row = to_z * 2 + to_y
        to_p = to_z * 4 + (to_y * 2 + to_core)
        remote(pot_send.at[row], pot_recv.at[p], pot_sems, (to_p, q)).start()
    own_pot = pltpu.make_async_copy(pot_send.at[z_low], pot_recv.at[p], own_sems.at[1])
    own_pot.start()

    loads[4].wait()
    for part in range(2):
        high, low = split(waves[part] * sphere)
        phi_s[0, :, part * LOCAL : part * LOCAL + LOCAL] = high
        phi_s[1, :, part * LOCAL : part * LOCAL + LOCAL] = low
    phi = pair(phi_s)
    turned = tuple(jnp.concatenate([-x[:, LOCAL:], x[:, :LOCAL]], axis=1) for x in phi)
    ca_send[:, 0] = product(phi, phi, True).reshape(NPY, 32, NB)
    ca_send[:, 1] = product(phi, turned, True).reshape(NPY, 32, NB)

    def send_corr_a(k, carry):
        to_q = partner_py(k, q)
        remote(ca_send.at[to_q], ca_recv.at[q], ca_sems, (p, to_q)).start()
        return carry

    lax.fori_loop(0, NPY - 1, send_corr_a, 0)
    own_ca = pltpu.make_async_copy(ca_send.at[q], ca_recv.at[q], own_sems.at[2])
    own_ca.start()

    loads[6].wait()
    pick_row = lax.broadcasted_iota(jnp.int32, (32, NB), 0)
    pick_lane = lax.broadcasted_iota(jnp.int32, (32, NB), 1)
    pick = jnp.where(lax.div(pick_lane, 8) == pick_row, 1.0, 0.0).astype(F32)
    wide = jnp.dot(
        coup[...].reshape(64, 32), pick, precision=lax.Precision.HIGHEST, preferred_element_type=F32
    )
    blk_j = lax.broadcasted_iota(jnp.int32, (8, 8, NB), 1)
    blk_lane = lax.broadcasted_iota(jnp.int32, (8, 8, NB), 2)
    wide = jnp.where(lax.rem(blk_lane, 8) == blk_j, wide.reshape(8, 8, NB), 0.0)
    wide = jnp.concatenate([jnp.sum(wide, axis=1)] * 32)
    sym_row = lax.broadcasted_iota(jnp.int32, (NB, NB), 0)
    sym_lane = lax.broadcasted_iota(jnp.int32, (NB, NB), 1)
    wide = jnp.where(lax.div(sym_row, 8) == lax.div(sym_lane, 8), wide, 0.0)
    high, low = split(0.5 * (wide + wide.T))
    for part in range(2):
        rows = slice(part * NB, part * NB + NB)
        store(mixed_s, part * NB, split(product((high, low), pair(beta_s, rows))))
    picked[...] = jnp.zeros((NPY * NG, NG), F32)

    own_forward.wait()
    wait_bytes(fwd_recv.at[pl.ds(0, NDEV - 1)], fwd_sems.at[1])
    proj_sum = jnp.zeros((NPX, NG), F32)
    for s in range(NPY):
        block = fwd_recv[s * NPX : s * NPX + NPX, :]
        proj_sum = proj_sum + block
        unpack[s * NG : s * NG + NG, :] = jnp.concatenate([block] * 4).T
    proj_sum = jnp.sum(proj_sum, axis=0, keepdims=True)
    proj_row = jnp.where((lane >= 64) & (lane < 96), proj_sum, 0.0)
    x_slot = lax.div(lane, 32).astype(F32) * 16.0
    y_slot = lax.broadcasted_iota(jnp.int32, (16, NPY, NG), 0).astype(F32)
    found = []
    for j in range(NCOLD):
        place = unpack[pl.ds(96 + j, NPY, stride=NG), :] - x_slot
        found.append(y_slot == place[None])
    for b in range(8):
        for part in range(2):
            plane = jnp.zeros((16, NPY, NG), F32)
            for j in range(NCOLD):
                value = unpack[pl.ds(part * 32 + j * 8 + b, NPY, stride=NG), :]
                plane = jnp.where(found[j], value[None], plane)
            field[part * NG : part * NG + NG, b * NG : b * NG + NG] = plane.reshape(NG, NG)

    own_pot.wait()
    wait_bytes(pot_recv.at[pl.ds(0, NPX - 1)], pot_sems.at[1])
    potential = pot_recv[...].reshape(NG, NG)
    potential = jnp.concatenate([potential, potential], axis=1)
    potential = jnp.concatenate([potential, potential])
    mat_a = pair(mats.at[pl.ds(0, 2)])
    mat_b = pair(mats.at[pl.ds(2, 2)])
    for c in range(4):
        two = slice(c * 256, c * 256 + 256)
        lines = product(mat_a, split(field[:, two]))
        for b in range(2):
            part = lines[:, b * NG : b * NG + NG]
            row = (2 * c + b) * NG
            store(lines_s, row, split(jnp.concatenate([part[:NG], part[NG:]], axis=1)))
    for c in range(4):
        two = slice(c * 256, c * 256 + 256)
        real = product(pair(lines_s, two), mat_b) * potential
        store(real_s, c * 256, split(real))
    for c in range(4):
        two = slice(c * 256, c * 256 + 256)
        back = product(pair(real_s, two), mat_a)
        columns = []
        for b in range(2):
            part = back[b * NG : b * NG + NG]
            columns.append(jnp.concatenate([part[:, :NG], part[:, NG:]]))
        store(lines_s, c * 256, split(jnp.concatenate(columns, axis=1)))
    for c in range(4):
        two = slice(c * 256, c * 256 + 256)
        grid[:, two] = product(mat_b, pair(lines_s, two))
    for b in range(8):
        for part in range(2):
            plane = grid[part * NG : part * NG + NG, b * NG : b * NG + NG].reshape(16, NPY, NG)
            for j in range(NCOLD):
                value = jnp.sum(jnp.where(found[j], plane, 0.0), axis=0)
                picked[pl.ds(part * 32 + j * 8 + b, NPY, stride=NG), :] = value
    for s in range(NPY):
        turned = picked[s * NG : s * NG + NG, :].T
        block = turned[0:32] + turned[32:64] + turned[64:96] + turned[96:128]
        back_send[s * NPX : s * NPX + NPX, :] = block + proj_row

    def send_back(to_z, to_y, to_core, to_q):
        to_p = to_z * 4 + (to_y * 2 + to_core)
        row = to_z * 4 + (to_q * NPX + to_y * 2 + to_core)
        remote(back_send.at[pl.ds(row, 1)], back_recv.at[pl.ds(owner, 1)], back_sems, (to_p, to_q)).start()

    each_other(p, q, send_back)
    own_back = pltpu.make_async_copy(back_send.at[pl.ds(slot, 1)], back_recv.at[pl.ds(owner, 1)], own_sems.at[3])
    own_back.start()

    own_ca.wait()
    wait_bytes(ca_recv.at[pl.ds(0, NPY - 1)], ca_sems.at[1])
    total = ca_recv[0]
    for s in range(1, NPY):
        total = total + ca_recv[s]
    total = total.reshape(64, NB)
    total = jnp.concatenate([total, jnp.zeros((64, NB), F32)])
    cb_send[...] = total.T.reshape(NPX, 8, NG)

    for to_z, to_y, to_core in along_px(p):
        to_p = to_z * 4 + (to_y * 2 + to_core)
        remote(cb_send.at[to_p], cb_recv.at[p], cb_sems, (to_p, q)).start()
    own_cb = pltpu.make_async_copy(cb_send.at[p], cb_recv.at[p], own_sems.at[4])
    own_cb.start()

    own_back.wait()
    wait_bytes(back_recv.at[pl.ds(0, NDEV - 1)], back_sems.at[1])
    low_rows = back_recv[0:NG, :]
    high_rows = back_recv[NG : 2 * NG, :]
    lines = jnp.where(lane < 64, low_rows, pltpu.roll(high_rows, 64, 1)).T
    lines = product(split(lines), pair(mats.at[pl.ds(2, 2)], slice(0, NG)))
    local_re = []
    local_im = []
    for h in range(2):
        res = [lines[h * 64 + j * 8 : h * 64 + j * 8 + 8] for j in range(4)]
        ims = [lines[h * 64 + 32 + j * 8 : h * 64 + 40 + j * 8] for j in range(4)]
        local_re.append(
            jnp.concatenate([r[:, :NG] + i[:, NG:] for r, i in zip(res, ims)], axis=1)
        )
        local_im.append(
            jnp.concatenate([i[:, :NG] - r[:, NG:] for r, i in zip(res, ims)], axis=1)
        )

    proj = jnp.concatenate([low_rows, high_rows])
    proj = pltpu.roll(proj, 64, 1).T[0:32]
    proj_re = proj[0:16]
    proj_im = proj[16:32]
    proj = jnp.concatenate(
        [
            jnp.concatenate([proj_re, -proj_im], axis=1),
            jnp.concatenate([proj_im, proj_re], axis=1),
        ]
    )
    high, low = split(proj)
    mixed = pair(mixed_s)
    stacked = jnp.dot(jnp.concatenate([high, low]), mixed[0], preferred_element_type=F32)
    nonlocal_part = jnp.dot(high, mixed[1], preferred_element_type=F32)
    nonlocal_part = stacked[0:32] + stacked[32:64] + nonlocal_part
    psi_re = waves[0, 0:BW, :] * sphere
    psi_im = waves[1, 0:BW, :] * sphere
    hpsi_re = kinetic * psi_re + sphere * jnp.concatenate(local_re) + nonlocal_part[0:16]
    hpsi_im = kinetic * psi_im + sphere * jnp.concatenate(local_im) + nonlocal_part[16:32]
    hpsi_ref[0] = hpsi_re
    hpsi_ref[1] = hpsi_im

    rows = []
    for h in range(2):
        re = hpsi_re[h * 8 : h * 8 + 8]
        im = hpsi_im[h * 8 : h * 8 + 8]
        rows.append(jnp.concatenate([re, im], axis=1))
        rows.append(jnp.concatenate([im, -re], axis=1))
    high, low = split(jnp.concatenate(rows))
    phi = pair(phi_s)
    dims = (((1,), (1,)), ((), ()))
    both = jnp.concatenate([high, low, jnp.zeros((64, 2 * LOCAL), BF16)])
    both = lax.dot_general(phi[0], both, dims, preferred_element_type=F32)
    high = jnp.concatenate([high, jnp.zeros((96, 2 * LOCAL), BF16)])
    rest = lax.dot_general(phi[1], high, dims, preferred_element_type=F32)
    ham[...] = both + pltpu.roll(both, 96, 1) + rest
    for h in range(2):
        block = jnp.zeros((NPX, NG), F32)
        for m in range(8):
            strip = pltpu.roll(ham[pl.ds(m, NPX, stride=8), :], (m - h) * 16 % NG, 1)
            block = jnp.where(lax.div(lane, 16) == m, strip, block)
        en_send[h * NPX : h * NPX + NPX, :] = block

    def send_energy(to_z, to_y, to_core, to_q):
        to_p = to_z * 4 + (to_y * 2 + to_core)
        row = to_z * 4 + (lax.div(to_q, 4) * NPX + to_y * 2 + to_core)
        remote(en_send.at[pl.ds(row, 1)], en_recv.at[pl.ds(slot, 1)], en_sems, (to_p, to_q)).start()

    each_other(p, q, send_energy)
    own_en = pltpu.make_async_copy(
        en_send.at[pl.ds(lax.div(q, 4) * NPX + p, 1)], en_recv.at[pl.ds(slot, 1)], own_sems.at[5]
    )
    own_en.start()

    scale = 1.0 / (NDEV * LOCAL)
    own_cb.wait()
    wait_bytes(cb_recv.at[pl.ds(0, NPX - 1)], cb_sems.at[1])
    total = jnp.sum(cb_recv[...], axis=0) * scale
    corr_ref[0] = total[:, 0:32]
    corr_ref[1] = total[:, 32:64]

    own_en.wait()
    wait_bytes(en_recv.at[pl.ds(0, NDEV - 1)], en_sems.at[1])
    total = jnp.zeros((NPX, NG), F32)
    for s in range(NPY):
        total = total + en_recv[s * NPX : s * NPX + NPX, :]
    total = jnp.sum(total, axis=0, keepdims=True) * scale
    m_row = lax.broadcasted_iota(jnp.int32, (8, NG), 0)
    m_lane = lax.broadcasted_iota(jnp.int32, (8, NG), 1)
    mine = jnp.where(lax.div(m_lane, 16) == m_row, total, 0.0)
    for part in range(2):
        n_first = part * 8 + lax.rem(q, 4) * 2
        for n in range(2):
            one = jnp.where(lax.rem(m_lane, 16) == n_first + n, mine, 0.0)
            energy_ref[part, n : n + 1, :] = jnp.sum(one, axis=1)[None]

    wait_bytes(fwd_send.at[pl.ds(0, NDEV - 1)], fwd_sems.at[0])
    wait_bytes(pot_recv.at[pl.ds(0, NPX - 1)], pot_sems.at[0])
    wait_bytes(ca_send.at[pl.ds(0, NPY - 1)], ca_sems.at[0])
    wait_bytes(cb_send.at[pl.ds(0, NPX - 1)], cb_sems.at[0])
    wait_bytes(back_send.at[pl.ds(0, NDEV - 1)], back_sems.at[0])
    wait_bytes(en_recv.at[pl.ds(0, NDEV - 1)], en_sems.at[0])


def finish(hpsi, corr, energy, hpsi_out, corr_out, energy_out, sems):
    pairs = ((hpsi, hpsi_out), (corr, corr_out), (energy, energy_out))
    copies = [pltpu.make_async_copy(a, b, sems.at[i]) for i, (a, b) in enumerate(pairs)]
    for copy in copies:
        copy.start()
    for copy in copies:
        copy.wait()


def body(waves, col_map, potential, projectors, coupling):
    vmem = pltpu.VMEM
    inside = pl.BlockSpec(memory_space=pltpu.VMEM)
    outside = pl.BlockSpec(memory_space=pltpu.HBM)
    mats = jnp.asarray(dft_tables())
    shapes = (
        jax.ShapeDtypeStruct((2, BW, LOCAL), F32),
        jax.ShapeDtypeStruct((2, 8, 32), F32),
        jax.ShapeDtypeStruct((2, 2, 8), F32),
    )
    arrays = (
        waves,
        col_map,
        jnp.transpose(potential, (1, 2, 0)),
        projectors,
        jnp.transpose(coupling, (1, 2, 0)),
        mats,
    )
    results = pl.pallas_call(
        kernel,
        out_shape=tuple(vmem(x.shape, x.dtype) for x in shapes),
        in_specs=[outside] * 6,
        out_specs=(inside, inside, inside),
        scratch_shapes=[
            vmem((2, NB, LOCAL), F32),
            vmem((2, NB, LOCAL), F32),
            vmem((4, 16, NG), F32),
            vmem((8, 8, 32), F32),
            vmem((2, NG, NG), F32),
            vmem((4, 256, 256), BF16),
            pltpu.SMEM((NCOLD,), jnp.int32),
            vmem((2, NB, 2 * LOCAL), BF16),
            vmem((2, 2 * NB, LOCAL), BF16),
            vmem((2, 2 * NB, LOCAL), BF16),
            vmem((NDEV, NG), F32),
            vmem((NDEV, NG), F32),
            vmem((16, 4, NG), F32),
            vmem((NPX, 4, NG), F32),
            vmem((NPY, 2, 32, NB), F32),
            vmem((NPY, 2, 32, NB), F32),
            vmem((NPX, 8, NG), F32),
            vmem((NPX, 8, NG), F32),
            vmem((NDEV, NG), F32),
            vmem((NDEV, NG), F32),
            vmem((2 * NPX, NG), F32),
            vmem((NDEV, NG), F32),
            vmem((NPY * NG, NG), F32),
            vmem((2 * NG, 8 * NG), F32),
            vmem((2 * NG, 8 * NG), F32),
            vmem((NPY * NG, NG), F32),
            vmem((NB, NG), F32),
            vmem((2, 8 * NG, 256), BF16),
            vmem((2, 8 * NG, 256), BF16),
            pltpu.SemaphoreType.DMA((7,)),
            pltpu.SemaphoreType.DMA((6,)),
            pltpu.SemaphoreType.DMA((2,)),
            pltpu.SemaphoreType.DMA((2,)),
            pltpu.SemaphoreType.DMA((2,)),
            pltpu.SemaphoreType.DMA((2,)),
            pltpu.SemaphoreType.DMA((2,)),
            pltpu.SemaphoreType.DMA((2,)),
        ],
        compiler_params=pltpu.CompilerParams(
            collective_id=0, has_side_effects=True, vmem_limit_bytes=40 << 20
        ),
        name="hamiltonian",
    )(*(pltpu.with_memory_space_constraint(x, pltpu.HBM) for x in arrays))
    hpsi, corr, energy = pl.pallas_call(
        finish,
        out_shape=shapes,
        in_specs=[inside] * 3,
        out_specs=(outside, outside, outside),
        scratch_shapes=[pltpu.SemaphoreType.DMA((3,))],
        name="finish",
    )(*(pltpu.with_memory_space_constraint(x, pltpu.VMEM) for x in results))
    return hpsi, corr, jnp.transpose(energy, (0, 2, 1))


def solution(mesh):
    placed = (
        P(None, None, ("px", "py")),
        P(("px", "py")),
        P(None, "px", "py"),
        P(None, None, ("px", "py")),
        P(),
    )
    return jax.shard_map(
        body,
        mesh=mesh,
        in_specs=placed,
        out_specs=(P(None, None, ("px", "py")), P(None, "px", "py"), P(None, "px", "py")),
        check_vma=False,
    )
```
